256 devices in a mesh: attn: 16 (over x, y), exp: 8 (over z), mb: 2 (over core).
Axes of the slice: x: 4, y: 4, z: 8, core: 2. Of those that a mesh axis runs over, the one named last changes fastest.
Arguments:
- resid: bfloat16 [2048, 6144], P(('attn', 'mb')), may hold values from -6 to 6
- norm_gain: bfloat16 [6144], replicated, may hold values from 0.099609375 to 1.8984375
- router: bfloat16 [6144, 8], replicated, may hold values from -0.078125 to 0.078125
- expert_ids: int32 [2048, 2], P(('attn', 'mb')), may hold values from 0 to 7, all different within a row; in each aligned block of 64 rows (0 to 63, 64 to 127, ...) at most 24 rows name the same one
- w_gate: bfloat16 [8, 6144, 8192], P('exp', None, ('attn', 'mb')), may hold values from -0.078125 to 0.078125
- w_up: bfloat16 [8, 6144, 8192], P('exp', None, ('attn', 'mb')), may hold values from -0.078125 to 0.078125
- w_down: bfloat16 [8, 8192, 6144], P('exp', ('attn', 'mb')), may hold values from -0.0625 to 0.0625
Outputs:
- mixed: bfloat16 [2048, 6144], P(('attn', 'mb'))
The draws below stay inside these ranges and needn't reach their ends.
Inputs may be any that keep to these rules, and one draw needn't show every extreme that they name: `expert_ids`: the two experts of a row differ. Among the rows of one device no expert is chosen by more than 24 rows, and some expert is chosen by exactly 24 of them.
All inputs are finite; a program needn't handle non-finite values.
Results may differ from the reference program's by a relative error of at most 0.012.
Values may be sent and summed in bfloat16 or wider, within the bound.
A program may use at most 128 MiB of HBM per device.

```python
import math
import jax
import jax.numpy as jnp
import numpy as np
from jax import lax

D = 6144
FF = 8192
EXPERTS = 8
ROWS = 64
CAP = 24
TOKENS = 2048
N_ATTN = 16
N_MB = 2


def shard_levels(stream_key, shape, pieces, low, largest):
    factor_of = 1.0
    for axis_at, parts in pieces:
        steps = jax.random.uniform(jax.random.fold_in(jax.random.fold_in(stream_key, 6), axis_at), (parts,), jnp.float32, low / len(pieces), largest / len(pieces))
        factor_of = factor_of * jnp.repeat(jnp.exp(steps), shape[axis_at] // parts).reshape((-1,) + (1,) * (len(shape) - 1 - axis_at))
    return factor_of


def routed_block(stream_key, own, number, rows, count, top, bound, lean):
    sequence = jax.random.permutation(stream_key, count)
    crowded, usual = portions_of(count, rows * top, bound, lean, True), portions_of(count, rows * top, bound, lean, False)
    places = jnp.arange(count)

    def named(lengths, rotation):
        used = int((lengths > 0).sum())
        fixed = max(1, used // 4)
        passed = fixed + (places - fixed + rotation * (used - fixed)) % max(1, count - fixed)
        return jnp.zeros((count,), jnp.int32).at[sequence[jnp.where(places < fixed, places, passed)]].set(jnp.asarray(lengths, jnp.int32))

    lengths = jnp.where(number % 4 == 0, named(crowded, number // 4), named(usual, number - number // 4 - 1))
    mixed = jax.random.permutation(jax.random.fold_in(own, 3), count)
    giver, taker = mixed[0:count // 2 * 2:2], mixed[1:count // 2 * 2:2]
    room = jnp.minimum(lengths[giver] - 1, bound - lengths[taker]) // 2
    room = jnp.where((giver == sequence[0]) | (taker == sequence[0]) | (lengths[taker] == 0), 0, jnp.maximum(room, 0))
    passed = jax.random.randint(jax.random.fold_in(own, 4), (count // 2,), 0, 1 << 20) % (room + 1)
    lengths = lengths.at[giver].add(-passed).at[taker].add(passed)
    members = jnp.searchsorted(jnp.cumsum(lengths), jnp.arange(rows * top), side="right").astype(jnp.int32)
    listing = members.reshape(top, rows).T
    listing = listing[jax.random.permutation(jax.random.fold_in(own, 1), rows)]
    rotation = jax.random.randint(jax.random.fold_in(own, 2), (rows, 1), 0, top)
    return jnp.take_along_axis(listing, (jnp.arange(top)[None, :] + rotation) % top, axis=1)


def portions_of(number_of, total, most, lean, full):
    loads = [(1 << 20) // math.isqrt(rank ** lean) + 1 for rank in range(1, number_of + 1)]
    largest = most if full else min(most, max(-(-total // number_of), total * loads[0] // sum(loads)))
    least = 1 if total - largest >= number_of - 1 else 0
    counts, surplus = [largest] + [least] * (number_of - 1), total - largest - least * (number_of - 1)
    while surplus > 0:
        movable = [i for i in range(1, number_of) if counts[i] < largest] or [i for i in range(1, number_of) if counts[i] < most]
        pool, remaining = sum([loads[i] for i in movable]), surplus
        for i in movable:
            addition = min(most - counts[i], max(1, remaining * loads[i] // pool), surplus)
            counts[i] = counts[i] + addition
            surplus = surplus - addition
    return np.array(counts)


def bell_draw(stream_key, dims, scale, limit, pieces=(), kind=jnp.bfloat16):
    gain = shard_levels(stream_key, dims, pieces, -0.22, 0.18) if pieces else 1.0
    result = jax.random.normal(stream_key, dims, jnp.float32) * scale * gain
    return jnp.minimum(jnp.maximum(result, -limit), limit).astype(kind)


def setup_inputs(seed: int = 0) -> dict:
    splits = jax.random.split(jax.random.key(seed), 8)
    resid = bell_draw(splits[0], (TOKENS, D), 1.0, 6.0, ((0, 32),))
    norm_gain = jnp.clip(1.0 + 0.18 * jax.random.normal(splits[1], (D,), jnp.float32), 0.099609375, 1.8984375).astype(jnp.bfloat16)
    router = bell_draw(splits[2], (D, EXPERTS), D ** -0.5, 0.078125)
    expert_ids_keys = jax.random.split(jax.random.fold_in(splits[3], 1), TOKENS // ROWS)
    expert_ids_turns = jax.random.permutation(jax.random.fold_in(splits[3], 3), TOKENS // ROWS)
    expert_ids = jax.vmap(lambda own, number: routed_block(jax.random.fold_in(splits[3], 2), own, number, ROWS, EXPERTS, 2, CAP, 2))(expert_ids_keys, expert_ids_turns).reshape((TOKENS, 2))
    w_gate = bell_draw(splits[4], (EXPERTS, D, FF), D ** -0.5, 0.078125, ((0, 8), (2, 32)))
    w_up = bell_draw(splits[5], (EXPERTS, D, FF), D ** -0.5, 0.078125, ((0, 8), (2, 32)))
    w_down = bell_draw(splits[6], (EXPERTS, FF, D), FF ** -0.5, 0.0625, ((0, 8), (1, 32)))
    return {"resid": resid, "norm_gain": norm_gain, "router": router, "expert_ids": expert_ids, "w_gate": w_gate, "w_up": w_up, "w_down": w_down}


def reference(resid, norm_gain, router, expert_ids, w_gate, w_up, w_down):
    floats = resid.astype(jnp.float32)
    scale = lax.rsqrt(lax.optimization_barrier(jnp.mean(floats * floats, axis=-1, keepdims=True)) + 1e-05)
    normed = (floats * scale * norm_gain.astype(jnp.float32)).astype(jnp.bfloat16)
    logits = jnp.dot(normed, router, preferred_element_type=jnp.float32)
    chosen = jnp.take_along_axis(logits, expert_ids, axis=1)
    first = jax.nn.sigmoid(chosen[:, 0] - chosen[:, 1])
    second = jax.nn.sigmoid(chosen[:, 1] - chosen[:, 0])
    pair_weights = jnp.stack([first, second], axis=1)
    blocks = N_ATTN * N_MB
    slots = blocks * CAP
    share = FF // blocks

    def per_expert(total, expert):
        hit = expert_ids == expert
        row_hit = jnp.any(hit, axis=1)
        count = jnp.sum(row_hit.astype(jnp.int32))
        index = jnp.nonzero(row_hit, size=slots, fill_value=0)[0].astype(jnp.int32)
        picked = normed[index]
        gate_w = w_gate[expert]
        up_w = w_up[expert]
        down_w = w_down[expert]
        gate = jnp.dot(picked, gate_w, preferred_element_type=jnp.float32)
        upper = jnp.dot(picked, up_w, preferred_element_type=jnp.float32)
        hidden = (jax.nn.silu(gate) * upper).astype(jnp.bfloat16)

        def add_block(acc, block):
            start = (block * share).astype(jnp.int32)
            piece = lax.dynamic_slice_in_dim(hidden, start, share, 1)
            rows_w = lax.dynamic_slice_in_dim(down_w, start, share, 0)
            part = jnp.dot(piece, rows_w, preferred_element_type=jnp.float32).astype(jnp.bfloat16)
            part = lax.optimization_barrier(part)
            return (acc + part.astype(jnp.float32), None)
        summed, _ = lax.scan(add_block, jnp.zeros((slots, D), jnp.float32), jnp.arange(blocks, dtype=jnp.int32))
        output = summed.astype(jnp.bfloat16)
        output = lax.optimization_barrier(output)
        weight = lax.optimization_barrier(jnp.sum(jnp.where(hit, pair_weights, jnp.float32(0.0)), axis=1))[index]
        valid = jnp.arange(slots, dtype=jnp.int32) < count
        weight = jnp.where(valid, weight, jnp.float32(0.0))
        total = total.at[index].add(weight[:, None] * output.astype(jnp.float32))
        return (total, None)
    start_total = jnp.zeros((resid.shape[0], D), jnp.float32)
    total, _ = lax.scan(per_expert, start_total, jnp.arange(EXPERTS, dtype=jnp.int32))
    return (floats + total).astype(jnp.bfloat16)
```

```python
import jax
import jax.numpy as jnp
from jax import lax
from jax.experimental import pallas as pl
from jax.experimental.pallas import tpu as pltpu
from jax.sharding import PartitionSpec as P

EXPERTS = 8
CAP = 24
ROWS = 64
D = 6144
HALF = D // 2
F = 256
SIDE = 4
LAYERS = 8
CHUNKS = 6
CW = D // CHUNKS
HW = CW // 2
OW = CW // LAYERS
STAGES = 7
MESH = pl.DeviceIdType.MESH
BF = jnp.bfloat16
F32 = jnp.float32


def dot(a, b):
    return jnp.dot(a, b, preferred_element_type=F32)


def kernel(
    resid_h, gain, router_t, ids, ids_t, wg_h, wu_h, wd_h, out_h,
    res, rows, wg, wu, wd, hid,
    p0, p1, p3, t1, t2, t3, qh, qf,
    v0, v1, v3, s1, s2, s3, ph, pf,
    eo, ec, table, om,
    load_sem, sib_send, sib_recv, a_send, a_recv,
    qh_send, qh_recv, qf_send, qf_recv, ph_send, ph_recv, pf_send, pf_recv,
    e_send, e_recv, o_send, o_recv, out_sem,
):
    attn, z, c = lax.axis_index("attn"), lax.axis_index("exp"), lax.axis_index("mb")
    x, y = attn // SIDE, attn % SIDE

    def plane(dx, dy):
        return {"attn": ((x + dx) % SIDE) * SIDE + (y + dy) % SIDE, "exp": z, "mb": c}

    def on_p(d):
        d = d % SIDE
        return plane((1 - c) * d, c * d)

    def on_q(d):
        d = d % SIDE
        return plane(c * d, (1 - c) * d)

    def on_z(d):
        return {"attn": attn, "exp": (z + d) % LAYERS, "mb": c}

    sibling = {"attn": attn, "exp": z, "mb": 1 - c}

    load_res = pltpu.make_async_copy(resid_h, res, load_sem.at[0])
    load_res.start()
    loads = [
        pltpu.make_async_copy(src.at[0], dst.at[0], load_sem.at[1 + i])
        for i, (src, dst) in enumerate(((wg_h, wg), (wu_h, wu), (wd_h, wd)))
    ]

    barrier = pltpu.get_barrier_semaphore()
    partners = [on_p(1), on_p(-1), on_q(1), on_q(-1), sibling] + [on_z(d) for d in range(1, LAYERS)]
    for device in partners:
        pl.semaphore_signal(barrier, inc=1, device_id=device, device_id_type=MESH)
    for load in loads:
        load.start()

    hit = ((ids_t[0:1, :] == z) | (ids_t[1:2, :] == z)).astype(F32)
    hits = jnp.broadcast_to(hit, (8, ROWS)).astype(BF)
    upper = (
        lax.broadcasted_iota(jnp.int32, (ROWS, ROWS), 0)
        < lax.broadcasted_iota(jnp.int32, (ROWS, ROWS), 1)
    ).astype(F32).astype(BF)
    rank = dot(hits, upper)[0:1, :]
    slot = lax.broadcasted_iota(jnp.int32, (CAP, ROWS), 0).astype(F32)
    pick = jnp.where((rank == slot) & (hit > 0.5), 1.0, 0.0).astype(BF)

    load_res.wait()
    square = jnp.zeros((CAP, CW), F32)
    for k in range(CHUNKS):
        cols = pl.ds(k * CW, CW)
        part = dot(pick, res[:, cols])
        t1_part = part.astype(BF)
        rows[0, 0, :, cols] = t1_part
        square = square + part * part
    scale = lax.rsqrt(jnp.sum(square, axis=1, keepdims=True) / D + 1e-05)
    for k in range(CHUNKS):
        cols = pl.ds(k * CW, CW)
        part = rows[0, 0, :, cols].astype(F32)
        rows[0, 0, :, cols] = (part * scale * gain[:, cols].astype(F32)).astype(BF)

    pl.semaphore_wait(barrier, len(partners))

    def remote(src, dst, send, recv, device):
        return pltpu.make_async_remote_copy(
            src_ref=src, dst_ref=dst, send_sem=send, recv_sem=recv,
            device_id=device, device_id_type=MESH,
        )

    sent = []

    def a_copy(pr, qr, to_pr, to_qr, half, device):
        n = len(sent)
        src, dst = rows.at[pr, qr], rows.at[to_pr, to_qr]
        if half is not None:
            part = pl.ds(half * HALF, HALF)
            src, dst = src.at[:, part], dst.at[:, part]
        copy = remote(src, dst, a_send.at[n], a_recv.at[to_pr, to_qr, half or 0], device)
        copy.start()
        sent.append(copy)

    def a_wait(pr, qr, halves=False):
        for half in range(2 if halves else 1):
            ref = rows.at[pr, qr]
            if halves:
                ref = ref.at[:, pl.ds(half * HALF, HALF)]
            remote(ref, ref, a_send.at[0], a_recv.at[pr, qr, half], sibling).wait_recv()

    a_copy(0, 0, 3, 0, None, on_p(1))
    a_copy(0, 0, 1, 0, None, on_p(-1))
    a_copy(0, 0, 0, 3, None, on_q(1))
    a_copy(0, 0, 0, 1, None, on_q(-1))

    siblings = []
    for i, (src, dst) in enumerate(((wg_h, wg), (wu_h, wu), (wd_h, wd))):
        copy = remote(src.at[0], dst.at[1], sib_send.at[i], sib_recv.at[i], sibling)
        copy.start()
        siblings.append(copy)

    square = jnp.zeros((ROWS, CW), F32)
    for k in range(CHUNKS):
        part = res[:, pl.ds(k * CW, CW)].astype(F32)
        square = square + part * part
    scale = lax.rsqrt(jnp.sum(square, axis=1, keepdims=True) / D + 1e-05)
    logits = jnp.zeros((ROWS, EXPERTS), F32)
    for k in range(CHUNKS):
        cols = pl.ds(k * CW, CW)
        normed = (res[:, cols].astype(F32) * scale * gain[:, cols].astype(F32)).astype(BF)
        logits = logits + lax.dot_general(
            normed, router_t[:, cols], (((1,), (1,)), ((), ())), preferred_element_type=F32
        )
    expert = lax.broadcasted_iota(jnp.int32, (ROWS, EXPERTS), 1)
    id_a, id_b = ids[:, 0:1], ids[:, 1:2]
    of_a = jnp.sum(jnp.where(expert == id_a, logits, 0.0), axis=1, keepdims=True)
    of_b = jnp.sum(jnp.where(expert == id_b, logits, 0.0), axis=1, keepdims=True)
    first, second = jax.nn.sigmoid(of_a - of_b), jax.nn.sigmoid(of_b - of_a)
    near = (expert + z) % EXPERTS
    chose_a, chose_b = near == id_a, near == id_b
    chosen = jnp.where(chose_a | chose_b, 1.0, 0.0)
    weight = jnp.where(chose_a, first, 0.0) + jnp.where(chose_b, second, 0.0)
    weight_hi = weight.astype(BF)
    weight_lo = (weight - weight_hi.astype(F32)).astype(BF)
    lower = (
        lax.broadcasted_iota(jnp.int32, (ROWS, ROWS), 0)
        > lax.broadcasted_iota(jnp.int32, (ROWS, ROWS), 1)
    ).astype(F32).astype(BF)
    ranks = dot(lower, chosen.astype(BF))
    wide = EXPERTS * CAP
    start = lax.broadcasted_iota(jnp.int32, (EXPERTS, wide), 0) * CAP
    lane = lax.broadcasted_iota(jnp.int32, (EXPERTS, wide), 1)
    spread = jnp.where((lane >= start) & (lane < start + CAP), 1.0, 0.0).astype(BF)
    place = (lax.broadcasted_iota(jnp.int32, (ROWS, wide), 1) % CAP).astype(F32)
    here = (dot(ranks.astype(BF), spread) == place) & (dot(chosen.astype(BF), spread) > 0.5)
    table[0:ROWS, :] = jnp.where(here, dot(weight_hi, spread), 0.0).astype(BF)
    table[ROWS:, :] = jnp.where(here, dot(weight_lo, spread), 0.0).astype(BF)

    def hidden(pr, s):
        lhs = rows[pr].reshape(SIDE * CAP, D)
        gate = dot(lhs, wg[s])
        upper_value = dot(lhs, wu[s])
        value = gate / (1.0 + jnp.exp(-gate)) * upper_value
        hid[pl.ds(pr * SIDE * CAP, SIDE * CAP), pl.ds(s * F, F)] = value.astype(BF)

    def forward_q(pr):
        a_wait(pr, 1)
        a_copy(pr, 1, pr, 2, 0, on_q(-1))
        a_wait(pr, 3)
        a_copy(pr, 3, pr, 2, 1, on_q(1))

    def spread_q(pr):
        a_copy(pr, 0, pr, 3, None, on_q(1))
        a_copy(pr, 0, pr, 1, None, on_q(-1))

    a_wait(1, 0)
    a_copy(1, 0, 2, 0, 0, on_p(-1))
    a_wait(3, 0)
    a_copy(3, 0, 2, 0, 1, on_p(1))
    forward_q(0)
    spread_q(1)
    spread_q(3)
    a_wait(2, 0, True)
    spread_q(2)
    a_wait(0, 2, True)
    loads[0].wait()
    loads[1].wait()
    hidden(0, 0)
    forward_q(1)
    siblings[0].wait_recv()
    siblings[1].wait_recv()
    hidden(0, 1)
    forward_q(3)
    a_wait(1, 2, True)
    hidden(1, 0)
    hidden(1, 1)
    forward_q(2)
    a_wait(3, 2, True)
    hidden(3, 0)
    hidden(3, 1)
    a_wait(2, 2, True)
    hidden(2, 0)
    hidden(2, 1)
    loads[2].wait()
    siblings[2].wait_recv()

    def ds_full(k):
        return pl.ds(pl.multiple_of(k * CW, CW), CW)

    def ds_half(k, half):
        return pl.ds(pl.multiple_of(k * CW + half * HW, HW), HW)

    def ds_pack(k):
        return pl.ds(pl.multiple_of(k * HW, HW), HW)

    def ds_own(k):
        return pl.ds(pl.multiple_of(k * OW, OW), OW)

    def ds_layer(k, layer):
        return pl.ds(pl.multiple_of(k * CW + layer * OW, OW), OW)

    def q_half(k, side):
        return remote(
            t2.at[:, :, ds_half(k, side)], qh.at[side, :, :, ds_pack(k)],
            qh_send.at[k, side], qh_recv.at[k, side], on_q(1 - 2 * side),
        )

    def q_full(k, side):
        return remote(
            (t1, t3)[side].at[:, :, ds_full(k)], qf.at[side, :, :, ds_full(k)],
            qf_send.at[k, side], qf_recv.at[k, side], on_q(1 - 2 * side),
        )

    def p_half(k, side):
        return remote(
            s2.at[:, ds_half(k, side)], ph.at[side, :, ds_pack(k)],
            ph_send.at[k, side], ph_recv.at[k, side], on_p(1 - 2 * side),
        )

    def p_full(k, side):
        return remote(
            (s1, s3)[side].at[:, ds_full(k)], pf.at[side, :, ds_full(k)],
            pf_send.at[k, side], pf_recv.at[k, side], on_p(1 - 2 * side),
        )

    def e_copy(k, d):
        return remote(
            eo.at[:, ds_layer(k, (z + d) % LAYERS)], ec.at[LAYERS - d, :, ds_own(k)],
            e_send.at[k, d - 1], e_recv.at[k, LAYERS - d - 1], on_z(d),
        )

    def e_arrived(k, d):
        return remote(
            eo.at[:, ds_layer(k, (z + d) % LAYERS)], ec.at[d, :, ds_own(k)],
            e_send.at[k, d - 1], e_recv.at[k, d - 1], on_z(d),
        )

    def o_copy(k, d):
        return remote(
            om.at[:, ds_layer(k, z)], om.at[:, ds_layer(k, z)],
            o_send.at[k, d - 1], o_recv.at[k, LAYERS - d - 1], on_z(d),
        )

    def o_arrived(k, d):
        there = om.at[:, ds_layer(k, (z + d) % LAYERS)]
        return remote(there, there, o_send.at[k, d - 1], o_recv.at[k, d - 1], on_z(d))

    def out_copy(k):
        return pltpu.make_async_copy(om.at[:, ds_full(k)], out_h.at[:, ds_full(k)], out_sem.at[k])

    def stage_down(k):
        cols = ds_full(k)
        value = dot(hid[:, 0:F], wd[0, :, cols]) + dot(hid[:, F:], wd[1, :, cols])
        value = value.reshape(SIDE, SIDE, CAP, CW)
        t2[:, :, cols] = value[:, 2].astype(BF)
        q_half(k, 0).start()
        q_half(k, 1).start()
        p0[:, :, cols] = value[:, 0]
        p1[:, :, cols] = value[:, 1]
        p3[:, :, cols] = value[:, 3]

    def stage_q_half(k):
        low, high, pack = ds_half(k, 0), ds_half(k, 1), ds_pack(k)
        q_half(k, 0).wait_recv()
        t1[:, :, low] = (p1[:, :, low] + qh[0, :, :, pack].astype(F32)).astype(BF)
        t1[:, :, high] = p1[:, :, high].astype(BF)
        q_full(k, 0).start()
        q_half(k, 1).wait_recv()
        t3[:, :, low] = p3[:, :, low].astype(BF)
        t3[:, :, high] = (p3[:, :, high] + qh[1, :, :, pack].astype(F32)).astype(BF)
        q_full(k, 1).start()

    def stage_q_full(k):
        cols = ds_full(k)
        q_full(k, 0).wait_recv()
        q_full(k, 1).wait_recv()

        def summed(pr):
            return p0[pr, :, cols] + qf[0, pr, :, cols].astype(F32) + qf[1, pr, :, cols].astype(F32)

        s2[:, cols] = summed(2).astype(BF)
        p_half(k, 0).start()
        p_half(k, 1).start()
        v1[:, cols] = summed(1)
        v3[:, cols] = summed(3)
        v0[:, cols] = summed(0)

    def stage_p_half(k):
        low, high, pack = ds_half(k, 0), ds_half(k, 1), ds_pack(k)
        p_half(k, 0).wait_recv()
        s1[:, low] = (v1[:, low] + ph[0, :, pack].astype(F32)).astype(BF)
        s1[:, high] = v1[:, high].astype(BF)
        p_full(k, 0).start()
        p_half(k, 1).wait_recv()
        s3[:, low] = v3[:, low].astype(BF)
        s3[:, high] = (v3[:, high] + ph[1, :, pack].astype(F32)).astype(BF)
        p_full(k, 1).start()

    def stage_p_full(k):
        cols = ds_full(k)
        p_full(k, 0).wait_recv()
        p_full(k, 1).wait_recv()
        total = v0[:, cols] + pf[0, :, cols].astype(F32) + pf[1, :, cols].astype(F32)
        eo[:, cols] = total.astype(BF)
        for d in range(1, LAYERS):
            e_copy(k, d).start()

    def stage_mix(k):
        mine = ds_layer(k, z)
        for d in range(1, LAYERS):
            e_arrived(k, d).wait_recv()
        ec[0, :, ds_own(k)] = eo[:, mine]
        every = ec[:, :, ds_own(k)].astype(F32).reshape(LAYERS * CAP, OW).astype(BF)
        both = dot(table[...], every)
        om[:, mine] = (res[:, mine].astype(F32) + (both[:ROWS] + both[ROWS:])).astype(BF)
        for d in range(1, LAYERS):
            o_copy(k, d).start()

    def stage_out(k):
        for d in range(1, LAYERS):
            o_arrived(k, d).wait_recv()
        out_copy(k).start()

    stages = [stage_down, stage_q_half, stage_q_full, stage_p_half, stage_p_full, stage_mix, stage_out]

    def step(i, carry):
        for s, stage in enumerate(stages):
            @pl.when((i >= s) & (i < s + CHUNKS))
            def _(s=s, stage=stage):
                stage(i - s)
        return carry

    lax.fori_loop(0, CHUNKS + STAGES - 1, step, 0)

    for copy in sent:
        copy.wait_send()
    for copy in siblings:
        copy.wait_send()

    def finish(k, carry):
        for side in range(2):
            q_half(k, side).wait_send()
            q_full(k, side).wait_send()
            p_half(k, side).wait_send()
            p_full(k, side).wait_send()
        for d in range(1, LAYERS):
            e_copy(k, d).wait_send()
            o_copy(k, d).wait_send()
        out_copy(k).wait()
        return carry

    lax.fori_loop(0, CHUNKS, finish, 0)


def per_device(resid, norm_gain, router, expert_ids, w_gate, w_up, w_down):
    vmem, hbm = pl.BlockSpec(memory_space=pltpu.VMEM), pl.BlockSpec(memory_space=pl.ANY)
    dma = pltpu.SemaphoreType.DMA
    block = (SIDE, CAP, D)
    return pl.pallas_call(
        kernel,
        name="expert_block",
        out_shape=jax.ShapeDtypeStruct((ROWS, D), BF),
        in_specs=[hbm, vmem, vmem, vmem, vmem, hbm, hbm, hbm],
        out_specs=hbm,
        scratch_shapes=[
            pltpu.VMEM((ROWS, D), BF),
            pltpu.VMEM((SIDE, SIDE, CAP, D), BF),
            pltpu.VMEM((2, D, F), BF),
            pltpu.VMEM((2, D, F), BF),
            pltpu.VMEM((2, F, D), BF),
            pltpu.VMEM((SIDE * SIDE * CAP, 2 * F), BF),
            pltpu.VMEM(block, F32),
            pltpu.VMEM(block, F32),
            pltpu.VMEM(block, F32),
            pltpu.VMEM(block, BF),
            pltpu.VMEM(block, BF),
            pltpu.VMEM(block, BF),
            pltpu.VMEM((2, SIDE, CAP, HALF), BF),
            pltpu.VMEM((2, SIDE, CAP, D), BF),
            pltpu.VMEM((CAP, D), F32),
            pltpu.VMEM((CAP, D), F32),
            pltpu.VMEM((CAP, D), F32),
            pltpu.VMEM((CAP, D), BF),
            pltpu.VMEM((CAP, D), BF),
            pltpu.VMEM((CAP, D), BF),
            pltpu.VMEM((2, CAP, HALF), BF),
            pltpu.VMEM((2, CAP, D), BF),
            pltpu.VMEM((CAP, D), BF),
            pltpu.VMEM((LAYERS, CAP, D // LAYERS), BF),
            pltpu.VMEM((2 * ROWS, EXPERTS * CAP), BF),
            pltpu.VMEM((ROWS, D), BF),
            dma((4,)),
            dma((3,)),
            dma((3,)),
            dma((20,)),
            dma((SIDE, SIDE, 2)),
        ]
        + [dma((CHUNKS, 2))] * 8
        + [dma((CHUNKS, LAYERS - 1))] * 4
        + [dma((CHUNKS,))],
        compiler_params=pltpu.CompilerParams(
            collective_id=0, has_side_effects=True, vmem_limit_bytes=60 * 1024 * 1024
        ),
    )(
        resid, norm_gain.reshape(1, D), router.T, expert_ids, expert_ids.T, w_gate, w_up, w_down
    )


def solution(mesh):
    in_specs = (
        P(("attn", "mb"), None),
        P(),
        P(),
        P(("attn", "mb"), None),
        P("exp", None, ("attn", "mb")),
        P("exp", None, ("attn", "mb")),
        P("exp", ("attn", "mb"), None),
    )
    out_specs = P(("attn", "mb"), None)
    return jax.shard_map(
        per_device, mesh=mesh, in_specs=in_specs, out_specs=out_specs, check_vma=False
    )
```

```python
import jax
import jax.numpy as jnp
from jax import lax
from jax.experimental import pallas as pl
from jax.experimental.pallas import tpu as pltpu
from jax.sharding import PartitionSpec as P

EXPERTS = 8
CAP = 24
ROWS = 64
D = 6144
HALF = D // 2
F = 256
SIDE = 4
LAYERS = 8
CHUNKS = 6
CW = D // CHUNKS
HW = CW // 2
OW = CW // LAYERS
LAGS = (0, 1, 2, 3, 4, 5)
ORDER = (
    (0, 0), (1, 0), (3, 0), (0, 1), (0, 3), (2, 0),
    (0, 2), (1, 1), (1, 3), (3, 1),
    (3, 3), (2, 1), (2, 3), (1, 2), (3, 2), (2, 2),
)
GROUPS = ((0, 6), (6, 10), (10, 16))
AT = {pair: n for n, pair in enumerate(ORDER)}
MESH = pl.DeviceIdType.MESH
BF = jnp.bfloat16
F32 = jnp.float32


def dot(a, b):
    return jnp.dot(a, b, preferred_element_type=F32)


def kernel(
    resid_h, gain_h, router_h, ids_h, wg_h, wu_h, wd_h, out_h,
    res, gain, router_t, ids, rows, wg, wu, wd, hid,
    p0, p1, p3, t1, t2, t3, qh, qf,
    v0, sp, pf,
    eo, ec, table, om,
    load_sem, sib_send, sib_recv, a_send, a_recv,
    b_send, qh_recv, qf_recv, pf_recv,
    e_recv, o_recv, out_sem,
):
    attn, z, c = lax.axis_index("attn"), lax.axis_index("exp"), lax.axis_index("mb")
    x, y = attn // SIDE, attn % SIDE

    def plane(dx, dy):
        return {"attn": ((x + dx) % SIDE) * SIDE + (y + dy) % SIDE, "exp": z, "mb": c}

    def on_p(d):
        d = d % SIDE
        return plane((1 - c) * d, c * d)

    def on_q(d):
        d = d % SIDE
        return plane(c * d, (1 - c) * d)

    def on_z(d):
        return {"attn": attn, "exp": (z + d) % LAYERS, "mb": c}

    sibling = {"attn": attn, "exp": z, "mb": 1 - c}

    barrier = pltpu.get_barrier_semaphore()
    partners = [on_p(1), on_p(-1), on_q(1), on_q(-1), sibling, on_p(2)]
    partners += [on_z(d) for d in range(1, LAYERS)]
    for device in partners:
        pl.semaphore_signal(barrier, inc=1, device_id=device, device_id_type=MESH)

    pairs = (
        (ids_h, ids), (resid_h, res), (gain_h, gain), (router_h, router_t),
        (wg_h.at[0], wg.at[0]), (wu_h.at[0], wu.at[0]), (wd_h.at[0], wd.at[0]),
    )
    loads = [pltpu.make_async_copy(src, dst, load_sem.at[i]) for i, (src, dst) in enumerate(pairs)]
    for load in loads:
        load.start()

    loads[0].wait()
    hit = ((ids[0:1, :] == z) | (ids[1:2, :] == z)).astype(F32)
    earlier = (
        lax.broadcasted_iota(jnp.int32, (ROWS, ROWS), 0)
        < lax.broadcasted_iota(jnp.int32, (ROWS, ROWS), 1)
    ).astype(F32).astype(BF)
    rank = dot(jnp.broadcast_to(hit, (8, ROWS)).astype(BF), earlier)[0:1, :]
    slot = lax.broadcasted_iota(jnp.int32, (CAP, ROWS), 0).astype(F32)
    pick = jnp.where((rank == slot) & (hit > 0.5), 1.0, 0.0).astype(BF)

    loads[1].wait()
    square = jnp.zeros((CAP, CW), F32)
    for k in range(CHUNKS):
        cols = pl.ds(k * CW, CW)
        part = dot(pick, res[:, cols])
        rows[0, :, cols] = part.astype(BF)
        square = square + part * part
    scale = lax.rsqrt(jnp.sum(square, axis=1, keepdims=True) / D + 1e-05)
    loads[2].wait()

    def gained(k):
        return gain[pl.ds(k * CW, CW)].astype(F32).reshape(1, CW)

    for k in range(CHUNKS):
        cols = pl.ds(k * CW, CW)
        part = rows[0, :, cols].astype(F32)
        rows[0, :, cols] = (part * scale * gained(k)).astype(BF)

    pl.semaphore_wait(barrier, len(partners))

    def remote(src, dst, send, recv, device):
        return pltpu.make_async_remote_copy(
            src_ref=src, dst_ref=dst, send_sem=send, recv_sem=recv,
            device_id=device, device_id_type=MESH,
        )

    def block(pr, qr, half=None):
        ref = rows.at[AT[pr, qr]]
        return ref if half is None else ref.at[:, pl.ds(half * HALF, HALF)]

    def a_copy(pr, qr, to_pr, to_qr, half, device):
        along_q = qr != to_qr
        remote(
            block(pr, qr, half), block(to_pr, to_qr, half),
            a_send.at[int(along_q)], a_recv.at[AT[to_pr, to_qr]], device,
        ).start()

    def a_wait(pr, qr):
        ref = block(pr, qr)
        remote(ref, ref, a_send.at[0], a_recv.at[AT[pr, qr]], sibling).wait_recv()

    a_copy(0, 0, 3, 0, None, on_p(1))
    a_copy(0, 0, 1, 0, None, on_p(-1))
    a_copy(0, 0, 0, 3, None, on_q(1))
    a_copy(0, 0, 0, 1, None, on_q(-1))

    siblings = []
    for i, (src, dst) in enumerate(((wg_h, wg), (wu_h, wu), (wd_h, wd))):
        copy = remote(src.at[0], dst.at[1], sib_send.at[i], sib_recv.at[i], sibling)
        copy.start()
        siblings.append(copy)

    square = jnp.zeros((ROWS, CW), F32)
    for k in range(CHUNKS):
        part = res[:, pl.ds(k * CW, CW)].astype(F32)
        square = square + part * part
    scale = lax.rsqrt(jnp.sum(square, axis=1, keepdims=True) / D + 1e-05)
    logits = jnp.zeros((ROWS, EXPERTS), F32)
    loads[3].wait()
    for k in range(CHUNKS):
        cols = pl.ds(k * CW, CW)
        normed = (res[:, cols].astype(F32) * scale * gained(k)).astype(BF)
        logits = logits + lax.dot_general(
            normed, router_t[:, cols], (((1,), (1,)), ((), ())), preferred_element_type=F32
        )
    expert = lax.broadcasted_iota(jnp.int32, (ROWS, EXPERTS), 1)
    unit = (
        lax.broadcasted_iota(jnp.int32, (ROWS, ROWS), 0)
        == lax.broadcasted_iota(jnp.int32, (ROWS, ROWS), 1)
    ).astype(F32).astype(BF)

    def upright(row):
        turned = lax.dot_general(
            unit, jnp.broadcast_to(row.astype(F32), (EXPERTS, ROWS)).astype(BF),
            (((1,), (1,)), ((), ())), preferred_element_type=F32,
        )
        return turned[:, 0:1].astype(jnp.int32)

    id_a, id_b = upright(ids[0:1, :]), upright(ids[1:2, :])
    near = (expert + z) % EXPERTS
    chose_a, chose_b = near == id_a, near == id_b
    chosen = jnp.where(chose_a | chose_b, 1.0, 0.0)
    lower = (
        lax.broadcasted_iota(jnp.int32, (ROWS, ROWS), 0)
        > lax.broadcasted_iota(jnp.int32, (ROWS, ROWS), 1)
    ).astype(F32).astype(BF)
    ranks = dot(lower, chosen.astype(BF))
    of_a = jnp.sum(jnp.where(expert == id_a, logits, 0.0), axis=1, keepdims=True)
    of_b = jnp.sum(jnp.where(expert == id_b, logits, 0.0), axis=1, keepdims=True)
    first, second = jax.nn.sigmoid(of_a - of_b), jax.nn.sigmoid(of_b - of_a)
    weight = jnp.where(chose_a, first, 0.0) + jnp.where(chose_b, second, 0.0)
    weight_hi = weight.astype(BF)
    weight_lo = (weight - weight_hi.astype(F32)).astype(BF)
    wide = EXPERTS * CAP
    start = lax.broadcasted_iota(jnp.int32, (EXPERTS, wide), 0) * CAP
    lane = lax.broadcasted_iota(jnp.int32, (EXPERTS, wide), 1)
    spread = jnp.where((lane >= start) & (lane < start + CAP), 1.0, 0.0).astype(BF)
    place = (lax.broadcasted_iota(jnp.int32, (ROWS, wide), 1) % CAP).astype(F32)
    here = (dot(ranks.astype(BF), spread) == place) & (dot(chosen.astype(BF), spread) > 0.5)
    table[0:ROWS, :] = jnp.where(here, dot(weight_hi, spread), 0.0).astype(BF)
    table[ROWS:, :] = jnp.where(here, dot(weight_lo, spread), 0.0).astype(BF)

    def hidden(group, s):
        low, high = GROUPS[group]
        lhs = rows[low:high].reshape((high - low) * CAP, D)
        gate = dot(lhs, wg[s])
        upper = dot(lhs, wu[s])
        value = gate / (1.0 + jnp.exp(-gate)) * upper
        hid[low * CAP : high * CAP, s * F : (s + 1) * F] = value.astype(BF)

    def forward_q(pr):
        a_wait(pr, 1)
        a_copy(pr, 1, pr, 2, 0, on_q(-1))
        a_wait(pr, 3)
        a_copy(pr, 3, pr, 2, 1, on_q(1))

    def spread_q(pr):
        a_copy(pr, 0, pr, 3, None, on_q(1))
        a_copy(pr, 0, pr, 1, None, on_q(-1))

    a_wait(1, 0)
    a_copy(1, 0, 2, 0, 0, on_p(-1))
    a_wait(3, 0)
    a_copy(3, 0, 2, 0, 1, on_p(1))
    forward_q(0)
    spread_q(1)
    spread_q(3)
    a_wait(2, 0)
    spread_q(2)
    loads[4].wait()
    loads[5].wait()
    hidden(0, 0)
    a_wait(0, 2)
    forward_q(1)
    siblings[0].wait_recv()
    siblings[1].wait_recv()
    hidden(0, 1)
    forward_q(3)
    hidden(1, 0)
    hidden(1, 1)
    forward_q(2)
    a_wait(1, 2)
    a_wait(3, 2)
    a_wait(2, 2)
    hidden(2, 0)
    hidden(2, 1)
    loads[6].wait()
    siblings[2].wait_recv()
    for copy in siblings:
        copy.wait_send()
    for along_q, ref in enumerate((rows.at[0:3], rows.at[0:12])):
        remote(ref, ref, a_send.at[along_q], a_recv.at[0], sibling).wait_send()

    def ds_full(k):
        return pl.ds(pl.multiple_of(k * CW, CW), CW)

    def ds_half(k, half):
        return pl.ds(pl.multiple_of(k * CW + half * HW, HW), HW)

    def ds_pack(k):
        return pl.ds(pl.multiple_of(k * HW, HW), HW)

    def ds_own(k):
        return pl.ds(pl.multiple_of(k * OW, OW), OW)

    def ds_layer(k, layer):
        return pl.ds(pl.multiple_of(k * CW + layer * OW, OW), OW)

    def q_half(k, side):
        return remote(
            t2.at[:, :, ds_half(k, side)], qh.at[side, :, :, ds_pack(k)],
            b_send.at[0], qh_recv.at[k], on_q(1 - 2 * side),
        )

    def q_full(k, side):
        return remote(
            (t1, t3)[side].at[:, :, ds_full(k)], qf.at[side, :, :, ds_full(k)],
            b_send.at[1], qf_recv.at[k], on_q(1 - 2 * side),
        )

    def p_copy(k, d):
        return remote(
            sp.at[d - 1, :, ds_full(k)], pf.at[SIDE - 1 - d, :, ds_full(k)],
            b_send.at[2], pf_recv.at[k], on_p(d),
        )

    def e_copy(k, d):
        return remote(
            eo.at[:, ds_layer(k, (z + d) % LAYERS)], ec.at[LAYERS - d, :, ds_own(k)],
            b_send.at[3], e_recv.at[k], on_z(d),
        )

    def o_copy(k, d):
        mine = om.at[:, ds_layer(k, z)]
        return remote(mine, mine, b_send.at[4], o_recv.at[k], on_z(d))

    def arrived(ref, sem):
        remote(ref, ref, b_send.at[0], sem, sibling).wait_recv()

    def left(ref, n):
        remote(ref, ref, b_send.at[n], out_sem.at[0], sibling).wait_send()

    def stage_down(k):
        cols = ds_full(k)
        value = dot(hid[:, 0:F], wd[0, :, cols]) + dot(hid[:, F:], wd[1, :, cols])
        value = value.reshape(SIDE * SIDE, CAP, CW)
        for pr in range(SIDE):
            t2[pr, :, cols] = value[AT[pr, 2]].astype(BF)
        q_half(k, 0).start()
        q_half(k, 1).start()
        for pr in range(SIDE):
            p0[pr, :, cols] = value[AT[pr, 0]]
            p1[pr, :, cols] = value[AT[pr, 1]]
            p3[pr, :, cols] = value[AT[pr, 3]]

    def stage_q_half(k):
        low, high, pack = ds_half(k, 0), ds_half(k, 1), ds_pack(k)
        arrived(qh.at[:, :, :, pack], qh_recv.at[k])
        t1[:, :, low] = (p1[:, :, low] + qh[0, :, :, pack].astype(F32)).astype(BF)
        t1[:, :, high] = p1[:, :, high].astype(BF)
        q_full(k, 0).start()
        t3[:, :, low] = p3[:, :, low].astype(BF)
        t3[:, :, high] = (p3[:, :, high] + qh[1, :, :, pack].astype(F32)).astype(BF)
        q_full(k, 1).start()

    def stage_q_full(k):
        cols = ds_full(k)
        arrived(qf.at[:, :, :, cols], qf_recv.at[k])

        def summed(pr):
            return p0[pr, :, cols] + qf[0, pr, :, cols].astype(F32) + qf[1, pr, :, cols].astype(F32)

        for d in (2, 1, 3):
            sp[d - 1, :, cols] = summed(d).astype(BF)
            p_copy(k, d).start()
        v0[:, cols] = summed(0)

    def stage_p(k):
        cols = ds_full(k)
        arrived(pf.at[:, :, cols], pf_recv.at[k])
        total = v0[:, cols]
        for n in range(SIDE - 1):
            total = total + pf[n, :, cols].astype(F32)
        eo[:, cols] = total.astype(BF)
        for d in range(1, LAYERS):
            e_copy(k, d).start()

    def stage_mix(k):
        mine = ds_layer(k, z)
        ec[0, :, ds_own(k)] = eo[:, mine]
        arrived(ec.at[1:LAYERS, :, ds_own(k)], e_recv.at[k])
        every = ec[:, :, ds_own(k)].astype(F32).reshape(LAYERS * CAP, OW).astype(BF)
        both = dot(table[...], every)
        om[:, mine] = (res[:, mine].astype(F32) + (both[:ROWS] + both[ROWS:])).astype(BF)
        for d in range(1, LAYERS):
            o_copy(k, d).start()

    def out_copy(k):
        return pltpu.make_async_copy(om.at[:, ds_full(k)], out_h.at[:, ds_full(k)], out_sem.at[0])

    def stage_out(k):
        arrived(om.at[:, pl.ds(pl.multiple_of(k * CW, CW), (LAYERS - 1) * OW)], o_recv.at[k])
        out_copy(k).start()

    stages = [stage_down, stage_q_half, stage_q_full, stage_p, stage_mix, stage_out]

    def step(i, carry):
        for s, stage in enumerate(stages):
            lag = LAGS[s]

            @pl.when((i >= lag) & (i < lag + CHUNKS))
            def _(lag=lag, stage=stage):
                stage(i - lag)
        return carry

    lax.fori_loop(0, CHUNKS + LAGS[-1], step, 0)

    left(t2, 0)
    left(qf, 1)
    left(pf, 2)
    left(ec.at[1:LAYERS], 3)
    left(om.at[:, 0 : (LAYERS - 1) * OW * CHUNKS], 4)
    pltpu.make_async_copy(om, out_h, out_sem.at[0]).wait()


def per_device(resid, norm_gain, router, expert_ids, w_gate, w_up, w_down):
    hbm = pl.BlockSpec(memory_space=pl.ANY)
    dma = pltpu.SemaphoreType.DMA
    block = (SIDE, CAP, D)
    return pl.pallas_call(
        kernel,
        name="expert_block",
        out_shape=jax.ShapeDtypeStruct((ROWS, D), BF),
        in_specs=[hbm] * 7,
        out_specs=hbm,
        scratch_shapes=[
            pltpu.VMEM((ROWS, D), BF),
            pltpu.VMEM((D,), BF),
            pltpu.VMEM((EXPERTS, D), BF),
            pltpu.VMEM((2, ROWS), jnp.int32),
            pltpu.VMEM((SIDE * SIDE, CAP, D), BF),
            pltpu.VMEM((2, D, F), BF),
            pltpu.VMEM((2, D, F), BF),
            pltpu.VMEM((2, F, D), BF),
            pltpu.VMEM((SIDE * SIDE * CAP, 2 * F), BF),
            pltpu.VMEM(block, F32),
            pltpu.VMEM(block, F32),
            pltpu.VMEM(block, F32),
            pltpu.VMEM(block, BF),
            pltpu.VMEM(block, BF),
            pltpu.VMEM(block, BF),
            pltpu.VMEM((2, SIDE, CAP, HALF), BF),
            pltpu.VMEM((2, SIDE, CAP, D), BF),
            pltpu.VMEM((CAP, D), F32),
            pltpu.VMEM((SIDE - 1, CAP, D), BF),
            pltpu.VMEM((SIDE - 1, CAP, D), BF),
            pltpu.VMEM((CAP, D), BF),
            pltpu.VMEM((LAYERS, CAP, D // LAYERS), BF),
            pltpu.VMEM((2 * ROWS, EXPERTS * CAP), BF),
            pltpu.VMEM((ROWS, D), BF),
            dma((7,)),
            dma((3,)),
            dma((3,)),
            dma((2,)),
            dma((SIDE * SIDE,)),
            dma((5,)),
        ]
        + [dma((CHUNKS,))] * 5
        + [dma((1,))],
        compiler_params=pltpu.CompilerParams(
            collective_id=0, has_side_effects=True, vmem_limit_bytes=60 * 1024 * 1024
        ),
    )(
        resid, norm_gain, router.T, expert_ids.T, w_gate, w_up, w_down
    )


def solution(mesh):
    in_specs = (
        P(("attn", "mb"), None),
        P(),
        P(),
        P(("attn", "mb"), None),
        P("exp", None, ("attn", "mb")),
        P("exp", None, ("attn", "mb")),
        P("exp", ("attn", "mb"), None),
    )
    out_specs = P(("attn", "mb"), None)
    return jax.shard_map(
        per_device, mesh=mesh, in_specs=in_specs, out_specs=out_specs, check_vma=False
    )
```

```python
import jax
import jax.numpy as jnp
from jax import lax
from jax.experimental import pallas as pl
from jax.experimental.pallas import tpu as pltpu
from jax.sharding import PartitionSpec as P

EXPERTS = 8
CAP = 24
ROWS = 64
D = 6144
HALF = D // 2
F = 256
SIDE = 4
LAYERS = 8
CHUNKS = 6
CW = D // CHUNKS
HW = CW // 2
OW = CW // LAYERS
LAGS = (0, 1, 2, 3, 4, 5)
LAST = CHUNKS - 1
FAR_FIRST = (4, 3, 5, 2, 6, 1, 7)
ORDER = (
    (0, 0), (1, 0), (3, 0), (0, 1), (0, 3), (2, 0),
    (0, 2), (1, 1), (1, 3), (3, 1),
    (3, 3), (2, 1), (2, 3), (1, 2), (3, 2), (2, 2),
)
GROUPS = ((0, 6), (6, 10), (10, 16))
AT = {pair: n for n, pair in enumerate(ORDER)}
MESH = pl.DeviceIdType.MESH
BF = jnp.bfloat16
F32 = jnp.float32


def dot(a, b):
    return jnp.dot(a, b, preferred_element_type=F32)


def kernel(
    resid_h, gain_h, router_h, ids_h, wg_h, wu_h, wd_h, out_h,
    res, gain, router_t, ids, rows, wg, wu, wd, hid,
    p0, p1, p3, t1, t2, t3, qh, qf, qd,
    v0, sp, pf,
    eo, ec, table, om,
    load_sem, sib_send, sib_recv, a_send, a_recv,
    b_send, qh_recv, qf_recv, pf_recv,
    e_recv, o_recv, out_sem,
):
    attn, z, c = lax.axis_index("attn"), lax.axis_index("exp"), lax.axis_index("mb")
    x, y = attn // SIDE, attn % SIDE

    def plane(dx, dy):
        return {"attn": ((x + dx) % SIDE) * SIDE + (y + dy) % SIDE, "exp": z, "mb": c}

    def on_p(d):
        d = d % SIDE
        return plane((1 - c) * d, c * d)

    def on_q(d):
        d = d % SIDE
        return plane(c * d, (1 - c) * d)

    def on_z(d):
        return {"attn": attn, "exp": (z + d) % LAYERS, "mb": c}

    sibling = {"attn": attn, "exp": z, "mb": 1 - c}

    barrier = pltpu.get_barrier_semaphore()
    partners = [on_p(1), on_p(-1), on_q(1), on_q(-1), sibling, on_p(2), on_q(2)]
    partners += [on_z(d) for d in range(1, LAYERS)]
    for device in partners:
        pl.semaphore_signal(barrier, inc=1, device_id=device, device_id_type=MESH)

    pairs = (
        (ids_h, ids), (resid_h, res), (gain_h, gain), (router_h, router_t),
        (wg_h.at[0], wg.at[0]), (wu_h.at[0], wu.at[0]), (wd_h.at[0], wd.at[0]),
    )
    loads = [pltpu.make_async_copy(src, dst, load_sem.at[i]) for i, (src, dst) in enumerate(pairs)]
    for load in loads:
        load.start()

    loads[0].wait()
    hit = ((ids[0:1, :] == z) | (ids[1:2, :] == z)).astype(F32)
    earlier = (
        lax.broadcasted_iota(jnp.int32, (ROWS, ROWS), 0)
        < lax.broadcasted_iota(jnp.int32, (ROWS, ROWS), 1)
    ).astype(F32).astype(BF)
    rank = dot(jnp.broadcast_to(hit, (8, ROWS)).astype(BF), earlier)[0:1, :]
    slot = lax.broadcasted_iota(jnp.int32, (CAP, ROWS), 0).astype(F32)
    pick = jnp.where((rank == slot) & (hit > 0.5), 1.0, 0.0).astype(BF)

    loads[1].wait()
    square = jnp.zeros((CAP, CW), F32)
    for k in range(CHUNKS):
        cols = pl.ds(k * CW, CW)
        part = dot(pick, res[:, cols])
        rows[0, :, cols] = part.astype(BF)
        square = square + part * part
    scale = lax.rsqrt(jnp.sum(square, axis=1, keepdims=True) / D + 1e-05)
    loads[2].wait()

    def gained(k):
        return gain[pl.ds(k * CW, CW)].astype(F32).reshape(1, CW)

    for k in range(CHUNKS):
        cols = pl.ds(k * CW, CW)
        part = rows[0, :, cols].astype(F32)
        rows[0, :, cols] = (part * scale * gained(k)).astype(BF)

    pl.semaphore_wait(barrier, len(partners))

    def remote(src, dst, send, recv, device):
        return pltpu.make_async_remote_copy(
            src_ref=src, dst_ref=dst, send_sem=send, recv_sem=recv,
            device_id=device, device_id_type=MESH,
        )

    def block(pr, qr, half):
        return rows.at[AT[pr, qr], :, pl.ds(half * HALF, HALF)]

    def a_copy(pr, qr, half, to_pr, to_qr, device):
        along_q = qr != to_qr
        remote(
            block(pr, qr, half), block(to_pr, to_qr, half),
            a_send.at[int(along_q)], a_recv.at[AT[to_pr, to_qr], half], device,
        ).start()

    def a_wait(pr, qr, half):
        ref = block(pr, qr, half)
        remote(ref, ref, a_send.at[0], a_recv.at[AT[pr, qr], half], sibling).wait_recv()

    for first in (0, 1):
        a_copy(0, 0, first, 1, 0, on_p(-1))
        a_copy(0, 0, 1 - first, 3, 0, on_p(1))
        a_copy(0, 0, first, 0, 1, on_q(-1))
        a_copy(0, 0, 1 - first, 0, 3, on_q(1))

    siblings = []
    for i, (src, dst) in enumerate(((wg_h, wg), (wu_h, wu), (wd_h, wd))):
        copy = remote(src.at[0], dst.at[1], sib_send.at[i], sib_recv.at[i], sibling)
        copy.start()
        siblings.append(copy)

    square = jnp.zeros((ROWS, CW), F32)
    for k in range(CHUNKS):
        part = res[:, pl.ds(k * CW, CW)].astype(F32)
        square = square + part * part
    scale = lax.rsqrt(jnp.sum(square, axis=1, keepdims=True) / D + 1e-05)
    logits = jnp.zeros((ROWS, EXPERTS), F32)
    loads[3].wait()
    for k in range(CHUNKS):
        cols = pl.ds(k * CW, CW)
        normed = (res[:, cols].astype(F32) * scale * gained(k)).astype(BF)
        logits = logits + lax.dot_general(
            normed, router_t[:, cols], (((1,), (1,)), ((), ())), preferred_element_type=F32
        )
    expert = lax.broadcasted_iota(jnp.int32, (ROWS, EXPERTS), 1)
    unit = (
        lax.broadcasted_iota(jnp.int32, (ROWS, ROWS), 0)
        == lax.broadcasted_iota(jnp.int32, (ROWS, ROWS), 1)
    ).astype(F32).astype(BF)

    def upright(row):
        turned = lax.dot_general(
            unit, jnp.broadcast_to(row.astype(F32), (EXPERTS, ROWS)).astype(BF),
            (((1,), (1,)), ((), ())), preferred_element_type=F32,
        )
        return turned[:, 0:1].astype(jnp.int32)

    id_a, id_b = upright(ids[0:1, :]), upright(ids[1:2, :])
    near = (expert + z) % EXPERTS
    chose_a, chose_b = near == id_a, near == id_b
    chosen = jnp.where(chose_a | chose_b, 1.0, 0.0)
    lower = (
        lax.broadcasted_iota(jnp.int32, (ROWS, ROWS), 0)
        > lax.broadcasted_iota(jnp.int32, (ROWS, ROWS), 1)
    ).astype(F32).astype(BF)
    ranks = dot(lower, chosen.astype(BF))
    of_a = jnp.sum(jnp.where(expert == id_a, logits, 0.0), axis=1, keepdims=True)
    of_b = jnp.sum(jnp.where(expert == id_b, logits, 0.0), axis=1, keepdims=True)
    first, second = jax.nn.sigmoid(of_a - of_b), jax.nn.sigmoid(of_b - of_a)
    weight = jnp.where(chose_a, first, 0.0) + jnp.where(chose_b, second, 0.0)
    weight_hi = weight.astype(BF)
    weight_lo = (weight - weight_hi.astype(F32)).astype(BF)
    wide = EXPERTS * CAP
    start = lax.broadcasted_iota(jnp.int32, (EXPERTS, wide), 0) * CAP
    lane = lax.broadcasted_iota(jnp.int32, (EXPERTS, wide), 1)
    spread = jnp.where((lane >= start) & (lane < start + CAP), 1.0, 0.0).astype(BF)
    place = (lax.broadcasted_iota(jnp.int32, (ROWS, wide), 1) % CAP).astype(F32)
    here = (dot(ranks.astype(BF), spread) == place) & (dot(chosen.astype(BF), spread) > 0.5)
    table[0:ROWS, :] = jnp.where(here, dot(weight_hi, spread), 0.0).astype(BF)
    table[ROWS:, :] = jnp.where(here, dot(weight_lo, spread), 0.0).astype(BF)

    def hidden(group, s):
        low, high = GROUPS[group]
        lhs = rows[low:high].reshape((high - low) * CAP, D)
        gate = dot(lhs, wg[s])
        upper = dot(lhs, wu[s])
        value = gate / (1.0 + jnp.exp(-gate)) * upper
        hid[low * CAP : high * CAP, s * F : (s + 1) * F] = value.astype(BF)

    def forward_q(pr):
        a_wait(pr, 1, 0)
        a_copy(pr, 1, 0, pr, 2, on_q(-1))
        a_wait(pr, 3, 1)
        a_copy(pr, 3, 1, pr, 2, on_q(1))

    def spread_q(pr, half):
        for side in (half, 1 - half):
            a_copy(pr, 0, half, pr, 1 + 2 * side, on_q(2 * side - 1))

    def a_rest(*blocks):
        for pr, qr, half in blocks:
            a_wait(pr, qr, half)

    a_wait(1, 0, 0)
    a_copy(1, 0, 0, 2, 0, on_p(-1))
    a_wait(3, 0, 1)
    a_copy(3, 0, 1, 2, 0, on_p(1))
    forward_q(0)
    spread_q(1, 0)
    spread_q(3, 1)
    a_wait(1, 0, 1)
    spread_q(1, 1)
    a_wait(3, 0, 0)
    spread_q(3, 0)
    a_wait(2, 0, 0)
    spread_q(2, 0)
    a_wait(2, 0, 1)
    spread_q(2, 1)
    loads[4].wait()
    loads[5].wait()
    a_rest((0, 1, 1), (0, 3, 0))
    hidden(0, 0)
    forward_q(1)
    siblings[0].wait_recv()
    siblings[1].wait_recv()
    hidden(0, 1)
    forward_q(3)
    a_rest((0, 2, 0), (0, 2, 1), (1, 1, 1), (1, 3, 0), (3, 1, 1))
    hidden(1, 0)
    forward_q(2)
    hidden(1, 1)
    a_rest((3, 3, 0), (2, 1, 1), (2, 3, 0))
    for pr in (1, 3, 2):
        a_rest((pr, 2, 0), (pr, 2, 1))
    hidden(2, 0)
    hidden(2, 1)
    loads[6].wait()
    siblings[2].wait_recv()
    for copy in siblings:
        copy.wait_send()
    for along_q, ref in enumerate((rows.at[0:3], rows.at[0:12])):
        remote(ref, ref, a_send.at[along_q], a_recv.at[0, 0], sibling).wait_send()

    def ds_full(k):
        return pl.ds(pl.multiple_of(k * CW, CW), CW)

    def ds_half(k, half):
        return pl.ds(pl.multiple_of(k * CW + half * HW, HW), HW)

    def ds_pack(k):
        return pl.ds(pl.multiple_of(k * HW, HW), HW)

    def ds_own(k):
        return pl.ds(pl.multiple_of(k * OW, OW), OW)

    def ds_layer(k, layer):
        return pl.ds(pl.multiple_of(k * CW + layer * OW, OW), OW)

    def q_half(k, side):
        return remote(
            t2.at[:, :, ds_half(k, side)], qh.at[side, :, :, ds_pack(k)],
            b_send.at[0], qh_recv.at[k], on_q(1 - 2 * side),
        )

    def q_full(k, side):
        return remote(
            (t1, t3)[side].at[:, :, ds_full(k)], qf.at[side, :, :, ds_full(k)],
            b_send.at[1], qf_recv.at[k], on_q(1 - 2 * side),
        )

    def at_end(k):
        return (k == 0) | (k == LAST)

    def q_direct(k):
        return remote(
            t2.at[:, :, ds_full(k)], qd.at[k // LAST], b_send.at[0], qh_recv.at[k], on_q(2)
        )

    def p_copy(k, d):
        return remote(
            sp.at[d - 1, :, ds_full(k)], pf.at[SIDE - 1 - d, :, ds_full(k)],
            b_send.at[2], pf_recv.at[k], on_p(d),
        )

    def e_copy(k, d):
        return remote(
            eo.at[:, ds_layer(k, (z + d) % LAYERS)], ec.at[LAYERS - d, :, ds_own(k)],
            b_send.at[3], e_recv.at[k], on_z(d),
        )

    def o_copy(k, d):
        mine = om.at[:, ds_layer(k, z)]
        return remote(mine, mine, b_send.at[4], o_recv.at[k], on_z(d))

    def arrived(ref, sem):
        remote(ref, ref, b_send.at[0], sem, sibling).wait_recv()

    def left(ref, n):
        remote(ref, ref, b_send.at[n], out_sem.at[0], sibling).wait_send()

    def stage_down(k):
        cols = ds_full(k)
        value = dot(hid[:, 0:F], wd[0, :, cols]) + dot(hid[:, F:], wd[1, :, cols])
        value = value.reshape(SIDE * SIDE, CAP, CW)
        for pr in range(SIDE):
            t2[pr, :, cols] = value[AT[pr, 2]].astype(BF)

        @pl.when(at_end(k))
        def _():
            q_direct(k).start()

        @pl.when(jnp.logical_not(at_end(k)))
        def _():
            q_half(k, 0).start()
            q_half(k, 1).start()

        for pr in range(SIDE):
            p1[pr, :, cols] = value[AT[pr, 1]]
            p3[pr, :, cols] = value[AT[pr, 3]]

        @pl.when(at_end(k))
        def _():
            t1[:, :, cols] = p1[:, :, cols].astype(BF)
            q_full(k, 0).start()
            t3[:, :, cols] = p3[:, :, cols].astype(BF)
            q_full(k, 1).start()

        for pr in range(SIDE):
            p0[pr, :, cols] = value[AT[pr, 0]]

    def stage_q_half(k):
        low, high, pack = ds_half(k, 0), ds_half(k, 1), ds_pack(k)

        @pl.when(jnp.logical_not(at_end(k)))
        def _():
            arrived(qh.at[:, :, :, pack], qh_recv.at[k])
            t1[:, :, low] = (p1[:, :, low] + qh[0, :, :, pack].astype(F32)).astype(BF)
            t1[:, :, high] = p1[:, :, high].astype(BF)
            q_full(k, 0).start()
            t3[:, :, low] = p3[:, :, low].astype(BF)
            t3[:, :, high] = (p3[:, :, high] + qh[1, :, :, pack].astype(F32)).astype(BF)
            q_full(k, 1).start()

    def stage_q_full(k):
        cols = ds_full(k)
        arrived(qf.at[:, :, :, cols], qf_recv.at[k])

        @pl.when(at_end(k))
        def _():
            arrived(qd.at[0], qh_recv.at[k])
            p0[:, :, cols] = p0[:, :, cols] + qd[k // LAST].astype(F32)

        def summed(pr):
            return p0[pr, :, cols] + qf[0, pr, :, cols].astype(F32) + qf[1, pr, :, cols].astype(F32)

        for d in (2, 1, 3):
            sp[d - 1, :, cols] = summed(d).astype(BF)
            p_copy(k, d).start()
        v0[:, cols] = summed(0)

    def stage_p(k):
        cols = ds_full(k)
        arrived(pf.at[:, :, cols], pf_recv.at[k])
        total = v0[:, cols]
        for n in range(SIDE - 1):
            total = total + pf[n, :, cols].astype(F32)
        eo[:, cols] = total.astype(BF)
        for d in FAR_FIRST:
            e_copy(k, d).start()

    def stage_mix(k):
        mine = ds_layer(k, z)
        ec[0, :, ds_own(k)] = eo[:, mine]
        arrived(ec.at[1:LAYERS, :, ds_own(k)], e_recv.at[k])
        every = ec[:, :, ds_own(k)].astype(F32).reshape(LAYERS * CAP, OW).astype(BF)
        both = dot(table[...], every)
        om[:, mine] = (res[:, mine].astype(F32) + (both[:ROWS] + both[ROWS:])).astype(BF)
        for d in FAR_FIRST:
            o_copy(k, d).start()

    def out_copy(k):
        return pltpu.make_async_copy(om.at[:, ds_full(k)], out_h.at[:, ds_full(k)], out_sem.at[0])

    def stage_out(k):
        arrived(om.at[:, pl.ds(pl.multiple_of(k * CW, CW), (LAYERS - 1) * OW)], o_recv.at[k])
        out_copy(k).start()

    stages = [stage_down, stage_q_half, stage_q_full, stage_p, stage_mix, stage_out]

    def step(i, carry):
        for s, stage in enumerate(stages):
            lag = LAGS[s]

            if s < 2:
                @pl.when((i >= lag) & (i < lag + CHUNKS))
                def _(lag=lag, stage=stage):
                    stage(i - lag)
            else:
                @pl.when((i >= lag) & (i < lag + LAST))
                def _(lag=lag, stage=stage):
                    stage(i - lag)

                @pl.when(i == lag + LAST - 1)
                def _(stage=stage):
                    stage(LAST)
        return carry

    lax.fori_loop(0, LAST + LAGS[-1], step, 0)

    left(t2, 0)
    left(qf, 1)
    left(pf, 2)
    left(ec.at[1:LAYERS], 3)
    left(om.at[:, 0 : (LAYERS - 1) * OW * CHUNKS], 4)
    pltpu.make_async_copy(om, out_h, out_sem.at[0]).wait()


def per_device(resid, norm_gain, router, expert_ids, w_gate, w_up, w_down):
    hbm = pl.BlockSpec(memory_space=pl.ANY)
    dma = pltpu.SemaphoreType.DMA
    block = (SIDE, CAP, D)
    return pl.pallas_call(
        kernel,
        name="expert_block",
        out_shape=jax.ShapeDtypeStruct((ROWS, D), BF),
        in_specs=[hbm] * 7,
        out_specs=hbm,
        scratch_shapes=[
            pltpu.VMEM((ROWS, D), BF),
            pltpu.VMEM((D,), BF),
            pltpu.VMEM((EXPERTS, D), BF),
            pltpu.VMEM((2, ROWS), jnp.int32),
            pltpu.VMEM((SIDE * SIDE, CAP, D), BF),
            pltpu.VMEM((2, D, F), BF),
            pltpu.VMEM((2, D, F), BF),
            pltpu.VMEM((2, F, D), BF),
            pltpu.VMEM((SIDE * SIDE * CAP, 2 * F), BF),
            pltpu.VMEM(block, F32),
            pltpu.VMEM(block, F32),
            pltpu.VMEM(block, F32),
            pltpu.VMEM(block, BF),
            pltpu.VMEM(block, BF),
            pltpu.VMEM(block, BF),
            pltpu.VMEM((2, SIDE, CAP, HALF), BF),
            pltpu.VMEM((2, SIDE, CAP, D), BF),
            pltpu.VMEM((2, SIDE, CAP, CW), BF),
            pltpu.VMEM((CAP, D), F32),
            pltpu.VMEM((SIDE - 1, CAP, D), BF),
            pltpu.VMEM((SIDE - 1, CAP, D), BF),
            pltpu.VMEM((CAP, D), BF),
            pltpu.VMEM((LAYERS, CAP, D // LAYERS), BF),
            pltpu.VMEM((2 * ROWS, EXPERTS * CAP), BF),
            pltpu.VMEM((ROWS, D), BF),
            dma((7,)),
            dma((3,)),
            dma((3,)),
            dma((2,)),
            dma((SIDE * SIDE, 2)),
            dma((5,)),
        ]
        + [dma((CHUNKS,))] * 5
        + [dma((1,))],
        compiler_params=pltpu.CompilerParams(
            collective_id=0, has_side_effects=True, vmem_limit_bytes=60 * 1024 * 1024
        ),
    )(
        resid, norm_gain, router.T, expert_ids.T, w_gate, w_up, w_down
    )


def solution(mesh):
    in_specs = (
        P(("attn", "mb"), None),
        P(),
        P(),
        P(("attn", "mb"), None),
        P("exp", None, ("attn", "mb")),
        P("exp", None, ("attn", "mb")),
        P("exp", ("attn", "mb"), None),
    )
    out_specs = P(("attn", "mb"), None)
    return jax.shard_map(
        per_device, mesh=mesh, in_specs=in_specs, out_specs=out_specs, check_vma=False
    )
```

```python
import jax
import jax.numpy as jnp
from jax import lax
from jax.experimental import pallas as pl
from jax.experimental.pallas import tpu as pltpu
from jax.sharding import PartitionSpec as P

EXPERTS = 8
CAP = 24
ROWS = 64
D = 6144
HALF = D // 2
F = 256
SIDE = 4
LAYERS = 8
PARTS = 6
PW = D // PARTS
CHUNKS = 12
CW = D // CHUNKS
HW = CW // 2
OW = 128
OWNERS = CW // OW
TURNS = LAYERS // OWNERS
LAGS = (0, 2, 4, 6, 8, 10, 16)
RELAYED = CHUNKS - 2
LAST = CHUNKS - 1
FAR_FIRST = (4, 3, 5, 2, 6, 1, 7)
ORDER = (
    (0, 0), (0, 1), (0, 3), (0, 2),
    (1, 0), (3, 0), (2, 0), (1, 1), (1, 3), (3, 1),
    (3, 3), (2, 1), (2, 3), (1, 2), (3, 2), (2, 2),
)
GROUPS = ((0, 4), (4, 10), (10, 16))
EARLY = 4 * CAP
STEPS = (0, 1, 3, 2)
EW = 2048
SPAN = EW // CW
AT = {pair: n for n, pair in enumerate(ORDER)}
MESH = pl.DeviceIdType.MESH
BF = jnp.bfloat16
F32 = jnp.float32


def dot(a, b):
    return jnp.dot(a, b, preferred_element_type=F32)


def kernel(
    resid_h, gain_h, router_h, ids_h, wg_h, wu_h, wd_h, out_h,
    res, gain, router_t, ids, rows, wg, wu, wd, hid,
    p0, p1, p3, t1, t2, t3, qh, qf, qd,
    v0, sp, pf,
    eo, ec, table, om,
    load_sem, sib_send, sib_recv, a_send, a_recv,
    b_send, qh_recv, qf_recv, pf_recv,
    e_recv, o_recv, early_recv, out_sem,
):
    attn, z, c = lax.axis_index("attn"), lax.axis_index("exp"), lax.axis_index("mb")
    x, y = attn // SIDE, attn % SIDE

    def plane(dx, dy):
        return {"attn": ((x + dx) % SIDE) * SIDE + (y + dy) % SIDE, "exp": z, "mb": c}

    def on_p(d):
        d = d % SIDE
        return plane((1 - c) * d, c * d)

    def on_q(d):
        d = d % SIDE
        return plane(c * d, (1 - c) * d)

    def on_z(d):
        return {"attn": attn, "exp": (z + d) % LAYERS, "mb": c}

    sibling = {"attn": attn, "exp": z, "mb": 1 - c}

    barrier = pltpu.get_barrier_semaphore()
    partners = [on_p(1), on_p(-1), on_q(1), on_q(-1), sibling, on_p(2), on_q(2)]
    partners += [on_z(d) for d in range(1, LAYERS)]
    for device in partners:
        pl.semaphore_signal(barrier, inc=1, device_id=device, device_id_type=MESH)

    pairs = (
        (ids_h, ids), (resid_h, res), (gain_h, gain), (router_h, router_t),
        (wg_h.at[0], wg.at[0]), (wu_h.at[0], wu.at[0]), (wd_h.at[0], wd.at[0]),
    )
    loads = [pltpu.make_async_copy(src, dst, load_sem.at[i]) for i, (src, dst) in enumerate(pairs)]
    for load in loads:
        load.start()

    loads[0].wait()
    hit = ((ids[0:1, :] == z) | (ids[1:2, :] == z)).astype(F32)
    earlier = (
        lax.broadcasted_iota(jnp.int32, (ROWS, ROWS), 0)
        < lax.broadcasted_iota(jnp.int32, (ROWS, ROWS), 1)
    ).astype(F32).astype(BF)
    rank = dot(jnp.broadcast_to(hit, (8, ROWS)).astype(BF), earlier)[0:1, :]
    slot = lax.broadcasted_iota(jnp.int32, (CAP, ROWS), 0).astype(F32)
    pick = jnp.where((rank == slot) & (hit > 0.5), 1.0, 0.0).astype(BF)

    loads[1].wait()
    square = jnp.zeros((CAP, PW), F32)
    for k in range(PARTS):
        cols = pl.ds(k * PW, PW)
        part = dot(pick, res[:, cols])
        rows[0, :, cols] = part.astype(BF)
        square = square + part * part
    scale = lax.rsqrt(jnp.sum(square, axis=1, keepdims=True) / D + 1e-05)
    loads[2].wait()

    def gained(k):
        return gain[pl.ds(k * PW, PW)].astype(F32).reshape(1, PW)

    for k in range(PARTS):
        cols = pl.ds(k * PW, PW)
        part = rows[0, :, cols].astype(F32)
        rows[0, :, cols] = (part * scale * gained(k)).astype(BF)

    pl.semaphore_wait(barrier, len(partners))

    def remote(src, dst, send, recv, device):
        return pltpu.make_async_remote_copy(
            src_ref=src, dst_ref=dst, send_sem=send, recv_sem=recv,
            device_id=device, device_id_type=MESH,
        )

    def block(pr, qr, half):
        return rows.at[AT[pr, qr], :, pl.ds(half * HALF, HALF)]

    def a_copy(pr, qr, half, to_pr, to_qr, device):
        along_q = qr != to_qr
        remote(
            block(pr, qr, half), block(to_pr, to_qr, half),
            a_send.at[int(along_q)], a_recv.at[AT[to_pr, to_qr], half], device,
        ).start()

    def a_wait(pr, qr, half):
        ref = block(pr, qr, half)
        remote(ref, ref, a_send.at[0], a_recv.at[AT[pr, qr], half], sibling).wait_recv()

    for first in (0, 1):
        a_copy(0, 0, first, 1, 0, on_p(-1))
        a_copy(0, 0, 1 - first, 3, 0, on_p(1))
        a_copy(0, 0, first, 0, 1, on_q(-1))
        a_copy(0, 0, 1 - first, 0, 3, on_q(1))

    siblings = []
    for i, (src, dst) in enumerate(((wg_h, wg), (wu_h, wu), (wd_h, wd))):
        copy = remote(src.at[0], dst.at[1], sib_send.at[i], sib_recv.at[i], sibling)
        copy.start()
        siblings.append(copy)

    square = jnp.zeros((ROWS, PW), F32)
    for k in range(PARTS):
        part = res[:, pl.ds(k * PW, PW)].astype(F32)
        square = square + part * part
    scale = lax.rsqrt(jnp.sum(square, axis=1, keepdims=True) / D + 1e-05)
    logits = jnp.zeros((ROWS, EXPERTS), F32)
    loads[3].wait()
    for k in range(PARTS):
        cols = pl.ds(k * PW, PW)
        normed = (res[:, cols].astype(F32) * scale * gained(k)).astype(BF)
        logits = logits + lax.dot_general(
            normed, router_t[:, cols], (((1,), (1,)), ((), ())), preferred_element_type=F32
        )
    expert = lax.broadcasted_iota(jnp.int32, (ROWS, EXPERTS), 1)
    unit = (
        lax.broadcasted_iota(jnp.int32, (ROWS, ROWS), 0)
        == lax.broadcasted_iota(jnp.int32, (ROWS, ROWS), 1)
    ).astype(F32).astype(BF)

    def upright(row):
        turned = lax.dot_general(
            unit, jnp.broadcast_to(row.astype(F32), (EXPERTS, ROWS)).astype(BF),
            (((1,), (1,)), ((), ())), preferred_element_type=F32,
        )
        return turned[:, 0:1].astype(jnp.int32)

    id_a, id_b = upright(ids[0:1, :]), upright(ids[1:2, :])
    near = (expert + z) % EXPERTS
    chose_a, chose_b = near == id_a, near == id_b
    chosen = jnp.where(chose_a | chose_b, 1.0, 0.0)
    lower = (
        lax.broadcasted_iota(jnp.int32, (ROWS, ROWS), 0)
        > lax.broadcasted_iota(jnp.int32, (ROWS, ROWS), 1)
    ).astype(F32).astype(BF)
    ranks = dot(lower, chosen.astype(BF))
    of_a = jnp.sum(jnp.where(expert == id_a, logits, 0.0), axis=1, keepdims=True)
    of_b = jnp.sum(jnp.where(expert == id_b, logits, 0.0), axis=1, keepdims=True)
    first, second = jax.nn.sigmoid(of_a - of_b), jax.nn.sigmoid(of_b - of_a)
    weight = jnp.where(chose_a, first, 0.0) + jnp.where(chose_b, second, 0.0)
    weight_hi = weight.astype(BF)
    weight_lo = (weight - weight_hi.astype(F32)).astype(BF)
    wide = EXPERTS * CAP
    start = lax.broadcasted_iota(jnp.int32, (EXPERTS, wide), 0) * CAP
    lane = lax.broadcasted_iota(jnp.int32, (EXPERTS, wide), 1)
    spread = jnp.where((lane >= start) & (lane < start + CAP), 1.0, 0.0).astype(BF)
    place = (lax.broadcasted_iota(jnp.int32, (ROWS, wide), 1) % CAP).astype(F32)
    here = (dot(ranks.astype(BF), spread) == place) & (dot(chosen.astype(BF), spread) > 0.5)
    table[0:ROWS, :] = jnp.where(here, dot(weight_hi, spread), 0.0).astype(BF)
    table[ROWS:, :] = jnp.where(here, dot(weight_lo, spread), 0.0).astype(BF)

    def hidden(group, s):
        low, high = GROUPS[group]
        lhs = rows[low:high].reshape((high - low) * CAP, D)
        gate = dot(lhs, wg[s])
        upper = dot(lhs, wu[s])
        value = gate / (1.0 + jnp.exp(-gate)) * upper
        hid[low * CAP : high * CAP, s * F : (s + 1) * F] = value.astype(BF)

    def forward_q(pr):
        a_wait(pr, 1, 0)
        a_copy(pr, 1, 0, pr, 2, on_q(-1))
        a_wait(pr, 3, 1)
        a_copy(pr, 3, 1, pr, 2, on_q(1))

    def spread_q(pr, half):
        for side in (half, 1 - half):
            a_copy(pr, 0, half, pr, 1 + 2 * side, on_q(2 * side - 1))

    def a_rest(*blocks):
        for pr, qr, half in blocks:
            a_wait(pr, qr, half)

    def ds_full(k):
        return pl.ds(pl.multiple_of(k * CW, CW), CW)

    def ds_half(k, half):
        return pl.ds(pl.multiple_of(k * CW + half * HW, HW), HW)

    def ds_pack(k):
        return pl.ds(pl.multiple_of(k * HW, HW), HW)

    def ds_own(k):
        return pl.ds(pl.multiple_of(k // TURNS * OW, OW), OW)

    def ds_layer(k, layer):
        return pl.ds(pl.multiple_of(k * CW + layer % OWNERS * OW, OW), OW)

    def q_half(k, side):
        return remote(
            t2.at[1:, :, ds_half(k, side)], qh.at[side, 1:, :, ds_pack(k)],
            b_send.at[0], qh_recv.at[k], on_q(1 - 2 * side),
        )

    def q_full(k, side):
        return remote(
            (t1, t3)[side].at[1:, :, ds_full(k)], qf.at[side, 1:, :, ds_full(k)],
            b_send.at[1], qf_recv.at[k], on_q(1 - 2 * side),
        )

    def early_half(k, side):
        src = t2.at[0, :, pl.ds(pl.multiple_of(k * EW + side * EW // 2, EW // 2), EW // 2)]
        dst = qh.at[side, 0, :, pl.ds(pl.multiple_of(k * EW // 2, EW // 2), EW // 2)]
        return remote(src, dst, b_send.at[0], early_recv.at[0, k], on_q(1 - 2 * side))

    def early_full(k, side):
        cols = pl.ds(pl.multiple_of(k * EW, EW), EW)
        return remote(
            (t1, t3)[side].at[0, :, cols], qf.at[side, 0, :, cols],
            b_send.at[1], early_recv.at[1, k], on_q(1 - 2 * side),
        )

    def at_end(k):
        return (k == 0) | (k == LAST)

    def q_direct(k):
        return remote(
            t2.at[1:, :, ds_full(k)], qd.at[k // LAST], b_send.at[0], qh_recv.at[k], on_q(2)
        )

    def p_copy(k, d):
        return remote(
            sp.at[d - 1, :, ds_full(k)], pf.at[SIDE - 1 - d, :, ds_full(k)],
            b_send.at[2], pf_recv.at[k], on_p(d),
        )

    def owner(k, layer=z):
        return layer // OWNERS == k % TURNS

    def e_copy(k, layer):
        return remote(
            eo.at[:, ds_layer(k, layer)], ec.at[(z + LAYERS - layer) % LAYERS, :, ds_own(k)],
            b_send.at[3], e_recv.at[k], {"attn": attn, "exp": layer, "mb": c},
        )

    def o_copy(k, d):
        mine = om.at[:, ds_layer(k, z)]
        return remote(mine, mine, b_send.at[4], o_recv.at[int(d not in (2, 6)), k], on_z(d))

    def arrived(ref, sem):
        remote(ref, ref, b_send.at[0], sem, sibling).wait_recv()

    def left(ref, n):
        remote(ref, ref, b_send.at[n], out_sem.at[0], sibling).wait_send()

    def down(part, cols):
        return dot(hid[part, 0:F], wd[0, :, cols]) + dot(hid[part, F:], wd[1, :, cols])

    def down_early(k, carry):
        cols = pl.ds(pl.multiple_of(k * EW, EW), EW)
        value = down(slice(0, EARLY), cols).reshape(SIDE, CAP, EW)
        t2[0, :, cols] = value[AT[0, 2]].astype(BF)
        early_half(k, 0).start()
        early_half(k, 1).start()
        p0[0, :, cols] = value[AT[0, 0]]
        p1[0, :, cols] = value[AT[0, 1]]
        p3[0, :, cols] = value[AT[0, 3]]
        return carry

    def add_early(k, carry):
        low = pl.ds(pl.multiple_of(k * EW, EW // 2), EW // 2)
        high = pl.ds(pl.multiple_of(k * EW + EW // 2, EW // 2), EW // 2)
        pack = pl.ds(pl.multiple_of(k * EW // 2, EW // 2), EW // 2)
        arrived(qh.at[:, 0, :, pack], early_recv.at[0, k])
        t1[0, :, low] = (p1[0, :, low] + qh[0, 0, :, pack].astype(F32)).astype(BF)
        t1[0, :, high] = p1[0, :, high].astype(BF)
        early_full(k, 0).start()
        t3[0, :, low] = p3[0, :, low].astype(BF)
        t3[0, :, high] = (p3[0, :, high] + qh[1, 0, :, pack].astype(F32)).astype(BF)
        early_full(k, 1).start()
        return carry

    def stage_down(k):
        cols = ds_full(k)
        value = down(slice(EARLY, None), cols).reshape(SIDE * (SIDE - 1), CAP, CW)

        def keep(ref, qr, kind):
            for n in range(1, SIDE):
                ref[n, :, cols] = value[AT[STEPS[n], qr] - SIDE].astype(kind)

        keep(t2, 2, BF)

        @pl.when(at_end(k))
        def _():
            q_direct(k).start()

        @pl.when(jnp.logical_not(at_end(k)))
        def _():
            q_half(k, 0).start()
            q_half(k, 1).start()

        keep(p1, 1, F32)
        keep(p3, 3, F32)

        @pl.when(at_end(k))
        def _():
            t1[1:, :, cols] = p1[1:, :, cols].astype(BF)
            q_full(k, 0).start()
            t3[1:, :, cols] = p3[1:, :, cols].astype(BF)
            q_full(k, 1).start()

        keep(p0, 0, F32)

    def stage_q_half(k):
        low, high, pack = ds_half(k, 0), ds_half(k, 1), ds_pack(k)

        @pl.when(jnp.logical_not(at_end(k)))
        def _():
            arrived(qh.at[:, 1:, :, pack], qh_recv.at[k])
            t1[1:, :, low] = (p1[1:, :, low] + qh[0, 1:, :, pack].astype(F32)).astype(BF)
            t1[1:, :, high] = p1[1:, :, high].astype(BF)
            q_full(k, 0).start()
            t3[1:, :, low] = p3[1:, :, low].astype(BF)
            t3[1:, :, high] = (p3[1:, :, high] + qh[1, 1:, :, pack].astype(F32)).astype(BF)
            q_full(k, 1).start()

    def stage_q_full(k):
        cols = ds_full(k)
        @pl.when(k % SPAN == 0)
        def _():
            wide = pl.ds(pl.multiple_of(k // SPAN * EW, EW), EW)
            arrived(qf.at[:, 0, :, wide], early_recv.at[1, k // SPAN])

        arrived(qf.at[:, 1:, :, cols], qf_recv.at[k])

        @pl.when(at_end(k))
        def _():
            arrived(qd.at[0], qh_recv.at[k])
            p0[1:, :, cols] = p0[1:, :, cols] + qd[k // LAST].astype(F32)

        def summed(n):
            return p0[n, :, cols] + qf[0, n, :, cols].astype(F32) + qf[1, n, :, cols].astype(F32)

        for n in (3, 1, 2):
            d = STEPS[n]
            sp[d - 1, :, cols] = summed(n).astype(BF)
            p_copy(k, d).start()
        v0[:, cols] = summed(0)

    def stage_p(k):
        cols = ds_full(k)
        arrived(pf.at[:, :, cols], pf_recv.at[k])
        total = v0[:, cols]
        for n in range(SIDE - 1):
            total = total + pf[n, :, cols].astype(F32)
        eo[:, cols] = total.astype(BF)
        for n in range(OWNERS):
            layer = k % TURNS * OWNERS + (z + OWNERS // 2 + n) % OWNERS

            @pl.when(layer != z)
            def _(layer=layer):
                e_copy(k, layer).start()

    def stage_mix(k):
        @pl.when(owner(k))
        def _():
            mine = ds_layer(k, z)
            ec[0, :, ds_own(k)] = eo[:, mine]
            arrived(ec.at[1:LAYERS, :, ds_own(k)], e_recv.at[k])
            every = ec[:, :, ds_own(k)].astype(F32).reshape(LAYERS * CAP, OW).astype(BF)
            both = dot(table[...], every)
            om[:, mine] = (res[:, mine].astype(F32) + (both[:ROWS] + both[ROWS:])).astype(BF)
            for d in (2, 6, 1, 7):
                o_copy(k, d).start()

            @pl.when(k >= RELAYED)
            def _():
                for d in (4, 3, 5):
                    o_copy(k, d).start()

    def out_copy(k):
        return pltpu.make_async_copy(om.at[:, ds_full(k)], out_h.at[:, ds_full(k)], out_sem.at[0])

    def o_arrived(k, layers, later):
        ref = om.at[:, pl.ds(pl.multiple_of(k * CW, CW), layers * OW)]
        arrived(ref, o_recv.at[later, k])

    def stage_relay(k):
        o_arrived(k, 2 // TURNS, 0)
        for sign in (1, -1):
            layer = (z + LAYERS - 2 * sign) % LAYERS

            @pl.when((k < RELAYED) & owner(k, layer))
            def _(sign=sign, layer=layer):
                part = om.at[:, ds_layer(k, layer)]
                half = part.at[pl.ds(ROWS // 4 * (1 - sign), ROWS // 2)]
                sem = o_recv.at[1, k]
                remote(part, part, b_send.at[4], sem, on_z(LAYERS + sign)).start()
                remote(half, half, b_send.at[4], sem, on_z(LAYERS + 2 * sign)).start()

    def stage_out(k):
        @pl.when(owner(k))
        def _():
            o_arrived(k, OWNERS - 1 - 2 // TURNS, 1)

        if TURNS > 1:
            @pl.when(jnp.logical_not(owner(k)))
            def _():
                o_arrived(k, OWNERS - 2 // TURNS, 1)

        out_copy(k).start()

    a_wait(1, 0, 0)
    a_copy(1, 0, 0, 2, 0, on_p(-1))
    a_wait(3, 0, 1)
    a_copy(3, 0, 1, 2, 0, on_p(1))
    forward_q(0)
    spread_q(1, 0)
    spread_q(3, 1)
    a_wait(1, 0, 1)
    spread_q(1, 1)
    a_wait(3, 0, 0)
    spread_q(3, 0)
    a_wait(2, 0, 0)
    spread_q(2, 0)
    a_wait(2, 0, 1)
    spread_q(2, 1)
    loads[4].wait()
    loads[5].wait()
    a_rest((0, 1, 1), (0, 3, 0), (0, 2, 0), (0, 2, 1))
    hidden(0, 0)
    forward_q(1)
    siblings[0].wait_recv()
    siblings[1].wait_recv()
    hidden(0, 1)
    forward_q(3)
    a_rest((1, 1, 1), (1, 3, 0), (3, 1, 1))
    hidden(1, 0)
    forward_q(2)
    loads[6].wait()
    siblings[2].wait_recv()
    lax.fori_loop(0, D // EW, down_early, 0)
    hidden(1, 1)
    a_rest((3, 3, 0), (2, 1, 1), (2, 3, 0))
    for pr in (1, 3, 2):
        a_rest((pr, 2, 0), (pr, 2, 1))
    lax.fori_loop(0, D // EW, add_early, 0)
    hidden(2, 0)
    hidden(2, 1)
    for copy in siblings:
        copy.wait_send()
    for along_q, ref in enumerate((rows.at[0:3], rows.at[0:12])):
        remote(ref, ref, a_send.at[along_q], a_recv.at[0, 0], sibling).wait_send()

    stages = [stage_down, stage_q_half, stage_q_full, stage_p, stage_mix, stage_relay, stage_out]

    def step(i, carry):
        for s, stage in enumerate(stages):
            lag = LAGS[s]

            if s < 2:
                @pl.when((i >= lag) & (i < lag + CHUNKS))
                def _(lag=lag, stage=stage):
                    stage(i - lag)
            else:
                @pl.when((i >= lag) & (i < lag + LAST))
                def _(lag=lag, stage=stage):
                    stage(i - lag)

                @pl.when(i == lag + LAST - 1)
                def _(stage=stage):
                    stage(LAST)
        return carry

    lax.fori_loop(0, LAST + LAGS[-1], step, 0)

    left(t2, 0)
    left(qf, 1)
    left(pf, 2)
    left(ec.at[1:LAYERS], 3)
    left(om.at[:, 0 : D // LAYERS * (LAYERS - 1)], 4)
    pltpu.make_async_copy(om, out_h, out_sem.at[0]).wait()


def per_device(resid, norm_gain, router, expert_ids, w_gate, w_up, w_down):
    hbm = pl.BlockSpec(memory_space=pl.ANY)
    dma = pltpu.SemaphoreType.DMA
    block = (SIDE, CAP, D)
    return pl.pallas_call(
        kernel,
        name="expert_block",
        out_shape=jax.ShapeDtypeStruct((ROWS, D), BF),
        in_specs=[hbm] * 7,
        out_specs=hbm,
        scratch_shapes=[
            pltpu.VMEM((ROWS, D), BF),
            pltpu.VMEM((D,), BF),
            pltpu.VMEM((EXPERTS, D), BF),
            pltpu.VMEM((2, ROWS), jnp.int32),
            pltpu.VMEM((SIDE * SIDE, CAP, D), BF),
            pltpu.VMEM((2, D, F), BF),
            pltpu.VMEM((2, D, F), BF),
            pltpu.VMEM((2, F, D), BF),
            pltpu.VMEM((SIDE * SIDE * CAP, 2 * F), BF),
            pltpu.VMEM(block, F32),
            pltpu.VMEM(block, F32),
            pltpu.VMEM(block, F32),
            pltpu.VMEM(block, BF),
            pltpu.VMEM(block, BF),
            pltpu.VMEM(block, BF),
            pltpu.VMEM((2, SIDE, CAP, HALF), BF),
            pltpu.VMEM((2, SIDE, CAP, D), BF),
            pltpu.VMEM((2, SIDE - 1, CAP, CW), BF),
            pltpu.VMEM((CAP, D), F32),
            pltpu.VMEM((SIDE - 1, CAP, D), BF),
            pltpu.VMEM((SIDE - 1, CAP, D), BF),
            pltpu.VMEM((CAP, D), BF),
            pltpu.VMEM((LAYERS, CAP, D // LAYERS), BF),
            pltpu.VMEM((2 * ROWS, EXPERTS * CAP), BF),
            pltpu.VMEM((ROWS, D), BF),
            dma((7,)),
            dma((3,)),
            dma((3,)),
            dma((2,)),
            dma((SIDE * SIDE, 2)),
            dma((5,)),
        ]
        + [dma((CHUNKS,))] * 4
        + [dma((2, CHUNKS)), dma((2, D // EW))]
        + [dma((1,))],
        compiler_params=pltpu.CompilerParams(
            collective_id=0, has_side_effects=True, vmem_limit_bytes=60 * 1024 * 1024
        ),
    )(
        resid, norm_gain, router.T, expert_ids.T, w_gate, w_up, w_down
    )


def solution(mesh):
    in_specs = (
        P(("attn", "mb"), None),
        P(),
        P(),
        P(("attn", "mb"), None),
        P("exp", None, ("attn", "mb")),
        P("exp", None, ("attn", "mb")),
        P("exp", ("attn", "mb"), None),
    )
    out_specs = P(("attn", "mb"), None)
    return jax.shard_map(
        per_device, mesh=mesh, in_specs=in_specs, out_specs=out_specs, check_vma=False
    )
```

```python
import jax
import jax.numpy as jnp
from jax import lax
from jax.experimental import pallas as pl
from jax.experimental.pallas import tpu as pltpu
from jax.sharding import PartitionSpec as P

EXPERTS = 8
CAP = 24
ROWS = 64
D = 6144
HALF = D // 2
F = 256
SIDE = 4
LAYERS = 8
PARTS = 6
PW = D // PARTS
CHUNKS = 12
CW = D // CHUNKS
HW = CW // 2
OW = 128
OWNERS = CW // OW
TURNS = LAYERS // OWNERS
LAGS = (0, 2, 4, 6, 8, 10, 16)
RELAYED = CHUNKS - 2
LAST = CHUNKS - 1
FAR_FIRST = (4, 3, 5, 2, 6, 1, 7)
ORDER = (
    (0, 0), (0, 1), (0, 3), (0, 2),
    (1, 0), (3, 0), (2, 0), (1, 1), (1, 3), (3, 1),
    (3, 3), (2, 1), (2, 3), (1, 2), (3, 2), (2, 2),
)
GROUPS = ((0, 4), (4, 10), (10, 16))
EARLY = 4 * CAP
STEPS = (0, 1, 3, 2)
EW = 2048
SPAN = EW // CW
AT = {pair: n for n, pair in enumerate(ORDER)}
MESH = pl.DeviceIdType.MESH
BF = jnp.bfloat16
F32 = jnp.float32


def dot(a, b):
    return jnp.dot(a, b, preferred_element_type=F32)


def kernel(
    resid_h, gain_h, router_h, ids_h, wg_h, wu_h, wd_h, out_h,
    res, gain, router_t, ids, rows, wg, wu, wd, hid,
    p0, p1, p3, t1, t2, t3, qh, qf, qd,
    v0, sp, pf,
    eo, ec, table, om,
    load_sem, sib_send, sib_recv, a_send, a_recv,
    b_send, qh_recv, qf_recv, pf_recv,
    e_recv, o_recv, early_recv, out_sem,
):
    attn, z, c = lax.axis_index("attn"), lax.axis_index("exp"), lax.axis_index("mb")
    x, y = attn // SIDE, attn % SIDE

    def plane(dx, dy):
        return {"attn": ((x + dx) % SIDE) * SIDE + (y + dy) % SIDE, "exp": z, "mb": c}

    def on_p(d):
        d = d % SIDE
        return plane((1 - c) * d, c * d)

    def on_q(d):
        d = d % SIDE
        return plane(c * d, (1 - c) * d)

    def on_z(d):
        return {"attn": attn, "exp": (z + d) % LAYERS, "mb": c}

    sibling = {"attn": attn, "exp": z, "mb": 1 - c}

    barrier = pltpu.get_barrier_semaphore()
    partners = [on_p(1), on_p(-1), on_q(1), on_q(-1), sibling, on_p(2), on_q(2)]
    partners += [on_z(d) for d in range(1, LAYERS)]
    for device in partners:
        pl.semaphore_signal(barrier, inc=1, device_id=device, device_id_type=MESH)

    pairs = (
        (ids_h, ids), (resid_h, res), (gain_h, gain), (router_h, router_t),
        (wg_h.at[0], wg.at[0]), (wu_h.at[0], wu.at[0]), (wd_h.at[0], wd.at[0]),
    )
    loads = [pltpu.make_async_copy(src, dst, load_sem.at[i]) for i, (src, dst) in enumerate(pairs)]
    for load in loads:
        load.start()

    loads[0].wait()
    hit = ((ids[0:1, :] == z) | (ids[1:2, :] == z)).astype(F32)
    earlier = (
        lax.broadcasted_iota(jnp.int32, (ROWS, ROWS), 0)
        < lax.broadcasted_iota(jnp.int32, (ROWS, ROWS), 1)
    ).astype(F32).astype(BF)
    rank = dot(jnp.broadcast_to(hit, (8, ROWS)).astype(BF), earlier)[0:1, :]
    slot = lax.broadcasted_iota(jnp.int32, (CAP, ROWS), 0).astype(F32)
    pick = jnp.where((rank == slot) & (hit > 0.5), 1.0, 0.0).astype(BF)

    loads[1].wait()
    square = jnp.zeros((CAP, PW), F32)
    for k in range(PARTS):
        cols = pl.ds(k * PW, PW)
        part = dot(pick, res[:, cols])
        rows[0, :, cols] = part.astype(BF)
        square = square + part * part
    scale = lax.rsqrt(jnp.sum(square, axis=1, keepdims=True) / D + 1e-05)
    loads[2].wait()

    def gained(k):
        return gain[pl.ds(k * PW, PW)].astype(F32).reshape(1, PW)

    for k in range(PARTS):
        cols = pl.ds(k * PW, PW)
        part = rows[0, :, cols].astype(F32)
        rows[0, :, cols] = (part * scale * gained(k)).astype(BF)

    pl.semaphore_wait(barrier, len(partners))

    def remote(src, dst, send, recv, device):
        return pltpu.make_async_remote_copy(
            src_ref=src, dst_ref=dst, send_sem=send, recv_sem=recv,
            device_id=device, device_id_type=MESH,
        )

    def block(pr, qr, half):
        return rows.at[AT[pr, qr], :, pl.ds(half * HALF, HALF)]

    def a_copy(pr, qr, half, to_pr, to_qr, device):
        along_q = qr != to_qr
        remote(
            block(pr, qr, half), block(to_pr, to_qr, half),
            a_send.at[int(along_q)], a_recv.at[AT[to_pr, to_qr], half], device,
        ).start()

    def a_wait(pr, qr, half):
        ref = block(pr, qr, half)
        remote(ref, ref, a_send.at[0], a_recv.at[AT[pr, qr], half], sibling).wait_recv()

    for first in (0, 1):
        a_copy(0, 0, first, 1, 0, on_p(-1))
        a_copy(0, 0, 1 - first, 3, 0, on_p(1))
        a_copy(0, 0, first, 0, 1, on_q(-1))
        a_copy(0, 0, 1 - first, 0, 3, on_q(1))

    siblings = []
    for i, (src, dst) in enumerate(((wg_h, wg), (wu_h, wu), (wd_h, wd))):
        copy = remote(src.at[0], dst.at[1], sib_send.at[i], sib_recv.at[i], sibling)
        copy.start()
        siblings.append(copy)

    square = jnp.zeros((ROWS, PW), F32)
    for k in range(PARTS):
        part = res[:, pl.ds(k * PW, PW)].astype(F32)
        square = square + part * part
    scale = lax.rsqrt(jnp.sum(square, axis=1, keepdims=True) / D + 1e-05)
    logits = jnp.zeros((ROWS, EXPERTS), F32)
    loads[3].wait()
    for k in range(PARTS):
        cols = pl.ds(k * PW, PW)
        normed = (res[:, cols].astype(F32) * scale * gained(k)).astype(BF)
        logits = logits + lax.dot_general(
            normed, router_t[:, cols], (((1,), (1,)), ((), ())), preferred_element_type=F32
        )
    expert = lax.broadcasted_iota(jnp.int32, (ROWS, EXPERTS), 1)
    unit = (
        lax.broadcasted_iota(jnp.int32, (ROWS, ROWS), 0)
        == lax.broadcasted_iota(jnp.int32, (ROWS, ROWS), 1)
    ).astype(F32).astype(BF)

    def upright(row):
        turned = lax.dot_general(
            unit, jnp.broadcast_to(row.astype(F32), (EXPERTS, ROWS)).astype(BF),
            (((1,), (1,)), ((), ())), preferred_element_type=F32,
        )
        return turned[:, 0:1].astype(jnp.int32)

    id_a, id_b = upright(ids[0:1, :]), upright(ids[1:2, :])
    near = (expert + z) % EXPERTS
    chose_a, chose_b = near == id_a, near == id_b
    chosen = jnp.where(chose_a | chose_b, 1.0, 0.0)
    lower = (
        lax.broadcasted_iota(jnp.int32, (ROWS, ROWS), 0)
        > lax.broadcasted_iota(jnp.int32, (ROWS, ROWS), 1)
    ).astype(F32).astype(BF)
    ranks = dot(lower, chosen.astype(BF))
    of_a = jnp.sum(jnp.where(expert == id_a, logits, 0.0), axis=1, keepdims=True)
    of_b = jnp.sum(jnp.where(expert == id_b, logits, 0.0), axis=1, keepdims=True)
    first, second = jax.nn.sigmoid(of_a - of_b), jax.nn.sigmoid(of_b - of_a)
    weight = jnp.where(chose_a, first, 0.0) + jnp.where(chose_b, second, 0.0)
    weight_hi = weight.astype(BF)
    weight_lo = (weight - weight_hi.astype(F32)).astype(BF)
    wide = EXPERTS * CAP
    start = lax.broadcasted_iota(jnp.int32, (EXPERTS, wide), 0) * CAP
    lane = lax.broadcasted_iota(jnp.int32, (EXPERTS, wide), 1)
    spread = jnp.where((lane >= start) & (lane < start + CAP), 1.0, 0.0).astype(BF)
    place = (lax.broadcasted_iota(jnp.int32, (ROWS, wide), 1) % CAP).astype(F32)
    here = (dot(ranks.astype(BF), spread) == place) & (dot(chosen.astype(BF), spread) > 0.5)
    table[0:ROWS, :] = jnp.where(here, dot(weight_hi, spread), 0.0).astype(BF)
    table[ROWS:, :] = jnp.where(here, dot(weight_lo, spread), 0.0).astype(BF)

    def hidden(group, s):
        low, high = GROUPS[group]
        lhs = rows[low:high].reshape((high - low) * CAP, D)
        gate = dot(lhs, wg[s])
        upper = dot(lhs, wu[s])
        value = gate / (1.0 + jnp.exp(-gate)) * upper
        hid[low * CAP : high * CAP, s * F : (s + 1) * F] = value.astype(BF)

    def forward_q(pr):
        a_wait(pr, 1, 0)
        a_copy(pr, 1, 0, pr, 2, on_q(-1))
        a_wait(pr, 3, 1)
        a_copy(pr, 3, 1, pr, 2, on_q(1))

    def spread_q(pr, half):
        for side in (half, 1 - half):
            a_copy(pr, 0, half, pr, 1 + 2 * side, on_q(2 * side - 1))

    def a_rest(*blocks):
        for pr, qr, half in blocks:
            a_wait(pr, qr, half)

    def ds_full(k):
        return pl.ds(pl.multiple_of(k * CW, CW), CW)

    def ds_half(k, half):
        return pl.ds(pl.multiple_of(k * CW + half * HW, HW), HW)

    def ds_pack(k):
        return pl.ds(pl.multiple_of(k * HW, HW), HW)

    def ds_own(k):
        return pl.ds(pl.multiple_of(k // TURNS * OW, OW), OW)

    def ds_layer(k, layer):
        return pl.ds(pl.multiple_of(k * CW + layer % OWNERS * OW, OW), OW)

    def q_half(k, side):
        return remote(
            t2.at[1:, :, ds_half(k, side)], qh.at[side, 1:, :, ds_pack(k)],
            b_send.at[0], qh_recv.at[k], on_q(1 - 2 * side),
        )

    def q_full(k, side):
        return remote(
            (t1, t3)[side].at[1:, :, ds_full(k)], qf.at[side, 1:, :, ds_full(k)],
            b_send.at[1], qf_recv.at[k], on_q(1 - 2 * side),
        )

    def early_half(k, side):
        src = t2.at[0, :, pl.ds(pl.multiple_of(k * EW + side * EW // 2, EW // 2), EW // 2)]
        dst = qh.at[side, 0, :, pl.ds(pl.multiple_of(k * EW // 2, EW // 2), EW // 2)]
        return remote(src, dst, b_send.at[0], early_recv.at[0, k], on_q(1 - 2 * side))

    def early_full(k, side):
        cols = pl.ds(pl.multiple_of(k * EW, EW), EW)
        return remote(
            (t1, t3)[side].at[0, :, cols], qf.at[side, 0, :, cols],
            b_send.at[1], early_recv.at[1, k], on_q(1 - 2 * side),
        )

    def at_end(k):
        return (k == 0) | (k == LAST)

    def q_direct(k):
        return remote(
            t2.at[1:, :, ds_full(k)], qd.at[k // LAST], b_send.at[0], qh_recv.at[k], on_q(2)
        )

    def p_copy(k, d):
        return remote(
            sp.at[d - 1, :, ds_full(k)], pf.at[SIDE - 1 - d, :, ds_full(k)],
            b_send.at[2], pf_recv.at[k], on_p(d),
        )

    def owner(k, layer=z):
        return layer // OWNERS == k % TURNS

    def e_copy(k, layer):
        return remote(
            eo.at[:, ds_layer(k, layer)], ec.at[(z + LAYERS - layer) % LAYERS, :, ds_own(k)],
            b_send.at[3], e_recv.at[k], {"attn": attn, "exp": layer, "mb": c},
        )

    def o_copy(k, d):
        mine = om.at[:, ds_layer(k, z)]
        return remote(mine, mine, b_send.at[4], o_recv.at[int(d not in (2, 6)), k], on_z(d))

    def arrived(ref, sem):
        remote(ref, ref, b_send.at[0], sem, sibling).wait_recv()

    def left(ref, n):
        remote(ref, ref, b_send.at[n], out_sem.at[0], sibling).wait_send()

    def down(part, cols):
        return dot(hid[part, 0:F], wd[0, :, cols]) + dot(hid[part, F:], wd[1, :, cols])

    def down_early(k, carry):
        cols = pl.ds(pl.multiple_of(k * EW, EW), EW)
        value = down(slice(0, EARLY), cols).reshape(SIDE, CAP, EW)
        t2[0, :, cols] = value[AT[0, 2]].astype(BF)
        early_half(k, 0).start()
        early_half(k, 1).start()
        p0[0, :, cols] = value[AT[0, 0]]
        p1[0, :, cols] = value[AT[0, 1]]
        p3[0, :, cols] = value[AT[0, 3]]
        return carry

    def add_early(k, carry):
        low = pl.ds(pl.multiple_of(k * EW, EW // 2), EW // 2)
        high = pl.ds(pl.multiple_of(k * EW + EW // 2, EW // 2), EW // 2)
        pack = pl.ds(pl.multiple_of(k * EW // 2, EW // 2), EW // 2)
        arrived(qh.at[:, 0, :, pack], early_recv.at[0, k])
        t1[0, :, low] = (p1[0, :, low] + qh[0, 0, :, pack].astype(F32)).astype(BF)
        t1[0, :, high] = p1[0, :, high].astype(BF)
        early_full(k, 0).start()
        t3[0, :, low] = p3[0, :, low].astype(BF)
        t3[0, :, high] = (p3[0, :, high] + qh[1, 0, :, pack].astype(F32)).astype(BF)
        early_full(k, 1).start()
        return carry

    def stage_down(k):
        cols = ds_full(k)
        value = down(slice(EARLY, None), cols).reshape(SIDE * (SIDE - 1), CAP, CW)

        def keep(ref, qr, kind):
            for n in range(1, SIDE):
                ref[n, :, cols] = value[AT[STEPS[n], qr] - SIDE].astype(kind)

        keep(t2, 2, BF)

        @pl.when(at_end(k))
        def _():
            q_direct(k).start()

        @pl.when(jnp.logical_not(at_end(k)))
        def _():
            q_half(k, 0).start()
            q_half(k, 1).start()

        keep(p1, 1, F32)
        keep(p3, 3, F32)

        @pl.when(at_end(k))
        def _():
            t1[1:, :, cols] = p1[1:, :, cols].astype(BF)
            q_full(k, 0).start()
            t3[1:, :, cols] = p3[1:, :, cols].astype(BF)
            q_full(k, 1).start()

        keep(p0, 0, F32)

    def stage_q_half(k):
        low, high, pack = ds_half(k, 0), ds_half(k, 1), ds_pack(k)

        @pl.when(jnp.logical_not(at_end(k)))
        def _():
            arrived(qh.at[:, 1:, :, pack], qh_recv.at[k])
            t1[1:, :, low] = (p1[1:, :, low] + qh[0, 1:, :, pack].astype(F32)).astype(BF)
            t1[1:, :, high] = p1[1:, :, high].astype(BF)
            q_full(k, 0).start()
            t3[1:, :, low] = p3[1:, :, low].astype(BF)
            t3[1:, :, high] = (p3[1:, :, high] + qh[1, 1:, :, pack].astype(F32)).astype(BF)
            q_full(k, 1).start()

    def stage_q_full(k):
        cols = ds_full(k)
        @pl.when(k % SPAN == 0)
        def _():
            wide = pl.ds(pl.multiple_of(k // SPAN * EW, EW), EW)
            arrived(qf.at[:, 0, :, wide], early_recv.at[1, k // SPAN])

        arrived(qf.at[:, 1:, :, cols], qf_recv.at[k])

        @pl.when(at_end(k))
        def _():
            arrived(qd.at[0], qh_recv.at[k])
            p0[1:, :, cols] = p0[1:, :, cols] + qd[k // LAST].astype(F32)

        def summed(n):
            return p0[n, :, cols] + qf[0, n, :, cols].astype(F32) + qf[1, n, :, cols].astype(F32)

        for n in (3, 1, 2):
            d = STEPS[n]
            sp[d - 1, :, cols] = summed(n).astype(BF)
            p_copy(k, d).start()
        v0[:, cols] = summed(0)

    def stage_p(k):
        cols = ds_full(k)
        arrived(pf.at[:, :, cols], pf_recv.at[k])
        total = v0[:, cols]
        for n in range(SIDE - 1):
            total = total + pf[n, :, cols].astype(F32)
        eo[:, cols] = total.astype(BF)
        for n in range(OWNERS):
            layer = k % TURNS * OWNERS + (z + OWNERS // 2 + n) % OWNERS

            @pl.when(layer != z)
            def _(layer=layer):
                e_copy(k, layer).start()

    def stage_mix(k):
        @pl.when(owner(k))
        def _():
            mine = ds_layer(k, z)
            ec[0, :, ds_own(k)] = eo[:, mine]
            arrived(ec.at[1:LAYERS, :, ds_own(k)], e_recv.at[k])
            every = ec[:, :, ds_own(k)].astype(F32).reshape(LAYERS * CAP, OW).astype(BF)
            both = dot(table[...], every)
            om[:, mine] = (both[:ROWS] + both[ROWS:]).astype(BF)
            for d in (2, 6, 1, 7):
                o_copy(k, d).start()

            @pl.when(k >= RELAYED)
            def _():
                for d in (4, 3, 5):
                    o_copy(k, d).start()

    def out_copy(k):
        return pltpu.make_async_copy(om.at[:, ds_full(k)], out_h.at[:, ds_full(k)], out_sem.at[0])

    def o_arrived(k, layers, later):
        ref = om.at[:, pl.ds(pl.multiple_of(k * CW, CW), layers * OW)]
        arrived(ref, o_recv.at[later, k])

    def stage_relay(k):
        o_arrived(k, 2 // TURNS, 0)
        for sign in (1, -1):
            layer = (z + LAYERS - 2 * sign) % LAYERS

            @pl.when((k < RELAYED) & owner(k, layer))
            def _(sign=sign, layer=layer):
                part = om.at[:, ds_layer(k, layer)]
                half = part.at[pl.ds(ROWS // 4 * (1 - sign), ROWS // 2)]
                sem = o_recv.at[1, k]
                remote(part, part, b_send.at[4], sem, on_z(LAYERS + sign)).start()
                remote(half, half, b_send.at[4], sem, on_z(LAYERS + 2 * sign)).start()

    def stage_out(k):
        @pl.when(owner(k))
        def _():
            o_arrived(k, OWNERS - 1 - 2 // TURNS, 1)

        if TURNS > 1:
            @pl.when(jnp.logical_not(owner(k)))
            def _():
                o_arrived(k, OWNERS - 2 // TURNS, 1)

        out_copy(k).start()

    a_wait(1, 0, 0)
    a_copy(1, 0, 0, 2, 0, on_p(-1))
    a_wait(3, 0, 1)
    a_copy(3, 0, 1, 2, 0, on_p(1))
    forward_q(0)
    spread_q(1, 0)
    spread_q(3, 1)
    a_wait(1, 0, 1)
    spread_q(1, 1)
    a_wait(3, 0, 0)
    spread_q(3, 0)
    a_wait(2, 0, 0)
    spread_q(2, 0)
    a_wait(2, 0, 1)
    spread_q(2, 1)
    loads[4].wait()
    loads[5].wait()
    a_rest((0, 1, 1), (0, 3, 0), (0, 2, 0), (0, 2, 1))
    hidden(0, 0)
    forward_q(1)
    siblings[0].wait_recv()
    siblings[1].wait_recv()
    hidden(0, 1)
    forward_q(3)
    a_rest((1, 1, 1), (1, 3, 0), (3, 1, 1))
    hidden(1, 0)
    forward_q(2)
    loads[6].wait()
    siblings[2].wait_recv()
    lax.fori_loop(0, D // EW, down_early, 0)
    hidden(1, 1)
    a_rest((3, 3, 0), (2, 1, 1), (2, 3, 0))
    for pr in (1, 3, 2):
        a_rest((pr, 2, 0), (pr, 2, 1))
    lax.fori_loop(0, D // EW, add_early, 0)
    hidden(2, 0)
    hidden(2, 1)
    for copy in siblings:
        copy.wait_send()
    for along_q, ref in enumerate((rows.at[0:3], rows.at[0:12])):
        remote(ref, ref, a_send.at[along_q], a_recv.at[0, 0], sibling).wait_send()

    stages = [stage_down, stage_q_half, stage_q_full, stage_p, stage_mix, stage_relay, stage_out]

    def step(i, carry):
        for s, stage in enumerate(stages):
            lag = LAGS[s]

            if s < 2:
                @pl.when((i >= lag) & (i < lag + CHUNKS))
                def _(lag=lag, stage=stage):
                    stage(i - lag)
            else:
                @pl.when((i >= lag) & (i < lag + LAST))
                def _(lag=lag, stage=stage):
                    stage(i - lag)

                @pl.when(i == lag + LAST - 1)
                def _(stage=stage):
                    stage(LAST)
        return carry

    lax.fori_loop(0, LAST + LAGS[-1], step, 0)

    left(t2, 0)
    left(qf, 1)
    left(pf, 2)
    left(ec.at[1:LAYERS], 3)
    left(om.at[:, 0 : D // LAYERS * (LAYERS - 1)], 4)
    pltpu.make_async_copy(om, out_h, out_sem.at[0]).wait()


def per_device(resid, norm_gain, router, expert_ids, w_gate, w_up, w_down):
    hbm = pl.BlockSpec(memory_space=pl.ANY)
    dma = pltpu.SemaphoreType.DMA
    block = (SIDE, CAP, D)
    total = pl.pallas_call(
        kernel,
        name="expert_block",
        out_shape=jax.ShapeDtypeStruct((ROWS, D), BF),
        in_specs=[hbm] * 7,
        out_specs=hbm,
        scratch_shapes=[
            pltpu.VMEM((ROWS, D), BF),
            pltpu.VMEM((D,), BF),
            pltpu.VMEM((EXPERTS, D), BF),
            pltpu.VMEM((2, ROWS), jnp.int32),
            pltpu.VMEM((SIDE * SIDE, CAP, D), BF),
            pltpu.VMEM((2, D, F), BF),
            pltpu.VMEM((2, D, F), BF),
            pltpu.VMEM((2, F, D), BF),
            pltpu.VMEM((SIDE * SIDE * CAP, 2 * F), BF),
            pltpu.VMEM(block, F32),
            pltpu.VMEM(block, F32),
            pltpu.VMEM(block, F32),
            pltpu.VMEM(block, BF),
            pltpu.VMEM(block, BF),
            pltpu.VMEM(block, BF),
            pltpu.VMEM((2, SIDE, CAP, HALF), BF),
            pltpu.VMEM((2, SIDE, CAP, D), BF),
            pltpu.VMEM((2, SIDE - 1, CAP, CW), BF),
            pltpu.VMEM((CAP, D), F32),
            pltpu.VMEM((SIDE - 1, CAP, D), BF),
            pltpu.VMEM((SIDE - 1, CAP, D), BF),
            pltpu.VMEM((CAP, D), BF),
            pltpu.VMEM((LAYERS, CAP, D // LAYERS), BF),
            pltpu.VMEM((2 * ROWS, EXPERTS * CAP), BF),
            pltpu.VMEM((ROWS, D), BF),
            dma((7,)),
            dma((3,)),
            dma((3,)),
            dma((2,)),
            dma((SIDE * SIDE, 2)),
            dma((5,)),
        ]
        + [dma((CHUNKS,))] * 4
        + [dma((2, CHUNKS)), dma((2, D // EW))]
        + [dma((1,))],
        compiler_params=pltpu.CompilerParams(
            collective_id=0, has_side_effects=True, vmem_limit_bytes=60 * 1024 * 1024
        ),
    )(
        resid, norm_gain, router.T, expert_ids.T, w_gate, w_up, w_down
    )
    return (resid.astype(F32) + total.astype(F32)).astype(BF)


def solution(mesh):
    in_specs = (
        P(("attn", "mb"), None),
        P(),
        P(),
        P(("attn", "mb"), None),
        P("exp", None, ("attn", "mb")),
        P("exp", None, ("attn", "mb")),
        P("exp", ("attn", "mb"), None),
    )
    out_specs = P(("attn", "mb"), None)
    return jax.shard_map(
        per_device, mesh=mesh, in_specs=in_specs, out_specs=out_specs, check_vma=False
    )
```
